512 devices in a mesh: freq: 16 (over x, y_lo, core), vis: 32 (over z, y_hi).
Axes of the slice: x: 4, y: 4 (y_hi: 2, y_lo: 2; y = y_hi * 2 + y_lo), z: 16, core: 2. Of those that a mesh axis runs over, the one named last changes fastest.
Arguments:
- model: bfloat16 [256, 4096], P('vis'), may hold values from -0.01171875 to 0.01171875
- beam: bfloat16 [16, 256, 1024], P('freq', 'vis'), may hold values from 0.25 to 1.75
- vis_obs: float32 [16, 32, 2, 2048], P('freq', 'vis'), may hold values from -6 to 6
- vis_uv: float32 [16, 32, 2, 2048], P('freq', 'vis'), may hold values from 0 to 64
- spectral: float32 [16, 32, 2048], P('freq', 'vis'), may hold values from -1 to 1
- vis_subgrid: int32 [16, 32, 2048], P('freq', 'vis'), may hold values from 0 to 1
- counts: int32 [16, 32], P('freq', 'vis'), may hold values from 512 to 2048, as said below
- uv_offsets: int32 [16, 32, 2, 2], P('freq', 'vis'), may hold values from -128 to 127
- w_planes: int32 [16, 32, 2], P('freq', 'vis'), may hold values from 0 to 31
Outputs:
- residual_vis: float32 [16, 32, 2, 2048], P('freq', 'vis')
- dirty: float32 [256, 4096], P('vis')
The draws below stay inside these ranges and needn't reach their ends.
Inputs may be any that keep to these rules, and one draw needn't show every extreme that they name: `counts`: each block has at least 512 live visibilities; some block is full.
All inputs are finite; a program needn't handle non-finite values.
Results may differ from the reference program's by a relative error of at most 0.008.
Values may be sent and summed in bfloat16 or wider, within the bound.
A program may use at most 64 MiB of HBM per device.

```python
import math
import jax
import jax.numpy as jnp
from jax import lax

FS = 1024
TAY = 4
S = 64
NS = 2
WPL = 32
NV = 2048
NIMG = 256
N_FREQ = 16
N_VIS = 32


def draw_counts(key, part):
    key = jax.random.fold_in(key, 7)
    first_key, second_key = jax.random.split(key)
    drawn = jax.random.randint(first_key, (N_FREQ * N_VIS,), NV // 4, NV + 1)
    chosen = jax.random.randint(second_key, (), 0, N_FREQ * N_VIS)
    flattened = jnp.where(jnp.arange(N_FREQ * N_VIS) == chosen, NV, drawn)
    return flattened.reshape(N_FREQ, N_VIS).astype(jnp.int32)


def set_ends(array, own_key, low, largest):
    longest = array.shape.index(max(array.shape))
    spots = []
    for shift in (0, 1):
        where = [jax.random.randint(jax.random.fold_in(own_key, axis), (), 0, length) for axis, length in enumerate(array.shape)]
        where[longest] = (where[longest] + shift) % array.shape[longest]
        spots.append(tuple(where))
    return array.at[spots[0]].set(low).at[spots[1]].set(largest)


def levels(key, extent, cuts, least, top_value):
    def one(dim, parts):
        steps = jax.random.uniform(jax.random.fold_in(jax.random.fold_in(key, 6), dim), (parts,), jnp.float32, least / len(cuts), top_value / len(cuts))
        return jnp.repeat(jnp.exp(steps), extent[dim] // parts).reshape((-1,) + (1,) * (len(extent) - dim - 1))

    loudness = one(*cuts[0])
    for cut in cuts[1:]:
        loudness = loudness * one(*cut)
    return loudness


def bell_draw(key, shape, width, reach, pieces=(), kind=jnp.bfloat16):
    entries = jax.random.normal(key, shape, jnp.float32) * width
    if len(pieces) > 0:
        entries = levels(key, shape, pieces, -0.22, 0.18) * entries
    return jnp.clip(entries, min=-reach, max=reach).astype(kind)


def setup_inputs(seed: int = 0) -> dict:
    streams_of = jax.random.split(jax.random.key(seed), 10)
    model = bell_draw(streams_of[0], (NIMG, TAY * FS), (NIMG * FS) ** -0.5, 0.01171875, ((0, 32),))
    beam = jnp.clip(1.0 + 0.15 * jax.random.normal(streams_of[1], (N_FREQ, NIMG, FS), jnp.float32), 0.25, 1.75).astype(jnp.bfloat16)
    vis_obs = bell_draw(streams_of[2], (N_FREQ, N_VIS, 2, NV), 1.0, 6.0, ((0, 16), (1, 32)), jnp.float32)
    vis_uv = jnp.clip(64.0 * jax.random.uniform(streams_of[3], (N_FREQ, N_VIS, 2, NV), jnp.float32) ** levels(streams_of[3], (N_FREQ, N_VIS, 2, NV), ((0, 16), (1, 32)), -0.2, 0.2), 0.0, 64.0)
    spectral = jnp.clip(jax.random.uniform(streams_of[4], (N_FREQ, N_VIS, NV), jnp.float32, -1.0, 1.0) * levels(streams_of[4], (N_FREQ, N_VIS, NV), ((0, 16), (1, 32)), -0.4, 0.0), -1.0, 1.0)
    vis_subgrid = set_ends(jax.random.randint(streams_of[5], (N_FREQ, N_VIS, NV), 0, NS), jax.random.fold_in(streams_of[5], 1), 0, NS - 1).astype(jnp.int32)
    counts = draw_counts(jax.random.fold_in(streams_of[9], 71), 0)
    uv_offsets = set_ends(jax.random.randint(streams_of[7], (N_FREQ, N_VIS, 2, NS), -(NIMG // 2), NIMG // 2), jax.random.fold_in(streams_of[7], 1), -(NIMG // 2), (NIMG // 2) - 1).astype(jnp.int32)
    w_planes = set_ends(jax.random.randint(streams_of[8], (N_FREQ, N_VIS, NS), 0, WPL), jax.random.fold_in(streams_of[8], 1), 0, WPL - 1).astype(jnp.int32)
    return {"model": model, "beam": beam, "vis_obs": vis_obs, "vis_uv": vis_uv, "spectral": spectral, "vis_subgrid": vis_subgrid, "counts": counts, "uv_offsets": uv_offsets, "w_planes": w_planes}


KERNEL_WIDTH = 0.5

def axis_table(cell_index, pixels, w_plane, modulus):
    linear = jnp.mod(cell_index[:, None] * pixels[None, :], modulus)
    wrap_mod = 2 * modulus * modulus
    quadratic = jnp.mod(w_plane * pixels * pixels, wrap_mod)
    fraction = linear.astype(jnp.float32) / modulus + (quadratic.astype(jnp.float32) / wrap_mod)[None, :]
    phases = -2.0 * math.pi * fraction
    return (jnp.cos(phases).astype(jnp.bfloat16), jnp.sin(phases).astype(jnp.bfloat16))

def kernel_table(position, members, cell_count):
    cell_pos = jnp.arange(cell_count, dtype=jnp.float32)
    offset_cells = position[None, :] - cell_pos[:, None]
    values = jnp.exp(offset_cells * offset_cells * (-0.5 / (KERNEL_WIDTH * KERNEL_WIDTH)))
    return (values * members[None, :]).astype(jnp.bfloat16)

def block_terms(weighted, observed, positions, spectrum, sub_ids, live_count, uv_shift, w_shift, norm_scale):
    cell_index = jnp.arange(S, dtype=jnp.int32) - S // 2
    m_pixels = jnp.arange(FS, dtype=jnp.int32) - FS // 2
    l_pixels = jnp.arange(NIMG, dtype=jnp.int32) - NIMG // 2
    ev_rows = []
    ev_cols = []
    eu_list = []
    for sub_index in range(NS):
        ev_real, ev_imag = axis_table(uv_shift[1, sub_index] + cell_index, m_pixels, w_shift[sub_index], FS)
        ev_rows = ev_rows + [ev_real, ev_imag]
        ev_cols.append(jnp.concatenate([ev_real, ev_imag], axis=1))
        eu_real, eu_imag = axis_table(uv_shift[0, sub_index] + cell_index, l_pixels, w_shift[sub_index], NIMG)
        eu_list.append(jnp.concatenate([eu_real, eu_imag], axis=0))
    ev_stack = jnp.concatenate(ev_rows, axis=0)
    projected = lax.dot_general(weighted.reshape(NIMG * TAY, FS), ev_stack, (((1,), (1,)), ((), ())), preferred_element_type=jnp.float32).astype(jnp.bfloat16)
    projected = projected.reshape(NIMG, TAY, NS, 2 * S)
    powers = jnp.stack([spectrum ** term_index for term_index in range(TAY)])
    live_mask = (jnp.arange(NV, dtype=jnp.int32) < live_count).astype(jnp.float32)
    predicted = jnp.zeros((2, NV), jnp.float32)
    ku_all = []
    kv_all = []
    for sub_index in range(NS):
        product = jnp.dot(eu_list[sub_index], projected[:, :, sub_index, :].reshape(NIMG, TAY * 2 * S), preferred_element_type=jnp.float32).reshape(2, S, TAY, 2, S)
        model_grid = jnp.stack([product[0, :, :, 0] - product[1, :, :, 1], product[0, :, :, 1] + product[1, :, :, 0]]).astype(jnp.bfloat16)
        members = (sub_ids == sub_index).astype(jnp.float32)
        ku_table = kernel_table(positions[0], members, S)
        kv_table = kernel_table(positions[1], members, S)
        cell_wide = jnp.dot(model_grid.reshape(2 * S * TAY, S), kv_table, preferred_element_type=jnp.float32).reshape(2, S, TAY, NV)
        ku_wide = ku_table.astype(jnp.float32)[None, :, None, :] * powers[None, None, :, :]
        predicted = predicted + lax.optimization_barrier(jnp.sum(cell_wide * ku_wide, axis=(1, 2)))
        ku_all.append(ku_wide)
        kv_all.append(kv_table)
    residual = live_mask[None, :] * (observed - predicted)
    sections = []
    for sub_index in range(NS):
        spread = (residual[:, None, None, :] * ku_all[sub_index]).astype(jnp.bfloat16).reshape(2 * S * TAY, NV)
        cell_sum = lax.dot_general(spread, kv_all[sub_index], (((1,), (1,)), ((), ())), preferred_element_type=jnp.float32).astype(jnp.bfloat16)
        side_prod = jnp.dot(cell_sum, ev_cols[sub_index], preferred_element_type=jnp.float32).reshape(2, S, TAY, 2, FS)
        back = jnp.stack([side_prod[0, :, :, 0] + side_prod[1, :, :, 1], side_prod[1, :, :, 0] - side_prod[0, :, :, 1]]).astype(jnp.bfloat16)
        sections.append(back.reshape(2 * S, TAY * FS))
    image = lax.dot_general(jnp.concatenate(eu_list, axis=0), jnp.concatenate(sections, axis=0), (((0,), (0,)), ((), ())), preferred_element_type=jnp.float32) * norm_scale
    return (residual, image)

def reference(model, beam, vis_obs, vis_uv, spectral, vis_subgrid, counts, uv_offsets, w_planes):
    norm_scale = 1.0 / (S * math.sqrt(N_FREQ * N_VIS * NS))

    def group_fn(group_index):
        gain_wide = jnp.tile(beam[group_index].astype(jnp.float32), (1, TAY))
        weighted = (model.astype(jnp.float32) * gain_wide).astype(jnp.bfloat16)

        def block_fn(running, block_index):
            residual, image = block_terms(weighted, vis_obs[group_index, block_index], vis_uv[group_index, block_index], spectral[group_index, block_index], vis_subgrid[group_index, block_index], counts[group_index, block_index], uv_offsets[group_index, block_index], w_planes[group_index, block_index], norm_scale)
            return (running + image, residual)
        running, residuals = lax.scan(block_fn, jnp.zeros((NIMG, TAY * FS), jnp.float32), jnp.arange(N_VIS, dtype=jnp.int32))
        return (residuals, running * gain_wide)
    residuals, images = lax.map(group_fn, jnp.arange(N_FREQ, dtype=jnp.int32))
    return (residuals, lax.optimization_barrier(jnp.sum(images, axis=0)))
```

```python
import functools
import math

import jax
import jax.numpy as jnp
import numpy as np
from jax import lax
from jax.experimental import pallas as pl
from jax.experimental.pallas import tpu as pltpu
from jax.sharding import PartitionSpec as P

S = 64
KERNEL_WIDTH = 0.5
MESH = pl.DeviceIdType.MESH


def greet(axis, n, me):
    barrier = pltpu.get_barrier_semaphore()

    def one(d, carry):
        pl.semaphore_signal(
            barrier, inc=1, device_id={axis: lax.rem(me + d, n)}, device_id_type=MESH
        )
        return carry

    lax.fori_loop(1, n, one, 0)
    pl.semaphore_wait(barrier, n - 1)


def exchange_kernel(axis, n, spread, in_ref, out_ref, send_sem, recv_sem, own_sem):
    me = lax.axis_index(axis)

    def copy(d):
        to = lax.rem(me + d, n)
        return pltpu.make_async_remote_copy(
            src_ref=in_ref.at[to] if spread else in_ref,
            dst_ref=out_ref.at[me],
            send_sem=send_sem.at[d],
            recv_sem=recv_sem.at[d],
            device_id={axis: to},
            device_id_type=MESH,
        )

    greet(axis, n, me)

    def begin(d, carry):
        copy(d).start()
        return carry

    lax.fori_loop(1, n, begin, 0)
    own = pltpu.make_async_copy(in_ref.at[me] if spread else in_ref, out_ref.at[me], own_sem)
    own.start()
    own.wait()

    def end(d, carry):
        frm = lax.rem(me - d + n, n)
        got = pltpu.make_async_remote_copy(
            src_ref=in_ref.at[frm] if spread else in_ref,
            dst_ref=out_ref.at[frm],
            send_sem=send_sem.at[d],
            recv_sem=recv_sem.at[d],
            device_id={axis: frm},
            device_id_type=MESH,
        )
        got.wait_recv()
        copy(d).wait_send()
        return carry

    lax.fori_loop(1, n, end, 0)


def exchange(array, axis, spread, collective_id):
    n = lax.axis_size(axis)
    block = array.shape[1:] if spread else array.shape
    return pl.pallas_call(
        functools.partial(exchange_kernel, axis, n, spread),
        out_shape=jax.ShapeDtypeStruct((n,) + block, array.dtype),
        in_specs=[pl.BlockSpec(memory_space=pltpu.VMEM)],
        out_specs=pl.BlockSpec(memory_space=pltpu.VMEM),
        scratch_shapes=[
            pltpu.SemaphoreType.DMA((n,)),
            pltpu.SemaphoreType.DMA((n,)),
            pltpu.SemaphoreType.DMA,
        ],
        compiler_params=pltpu.CompilerParams(
            collective_id=collective_id, has_side_effects=True
        ),
    )(array)


def freq_sum_kernel(n, in_ref, out_ref, parts, total, send_sem, recv_sem, send2, recv2, own_sem):
    me = lax.axis_index("freq")
    greet("freq", n, me)

    def first(d, to):
        return pltpu.make_async_remote_copy(
            src_ref=in_ref.at[to],
            dst_ref=parts.at[d],
            send_sem=send_sem.at[d],
            recv_sem=recv_sem.at[d],
            device_id={"freq": to},
            device_id_type=MESH,
        )

    def second(d, to, slot):
        return pltpu.make_async_remote_copy(
            src_ref=total,
            dst_ref=out_ref.at[slot],
            send_sem=send2.at[d],
            recv_sem=recv2.at[d],
            device_id={"freq": to},
            device_id_type=MESH,
        )

    def begin(d, carry):
        first(d, lax.rem(me + d, n)).start()
        return carry

    lax.fori_loop(1, n, begin, 0)
    total[...] = in_ref[me]

    def take(d, carry):
        first(d, lax.rem(me - d + n, n)).wait_recv()
        total[...] += parts[d]
        return carry

    lax.fori_loop(1, n, take, 0)

    def tell(d, carry):
        second(d, lax.rem(me + d, n), me).start()
        return carry

    lax.fori_loop(1, n, tell, 0)
    own = pltpu.make_async_copy(total, out_ref.at[me], own_sem)
    own.start()
    own.wait()

    def end(d, carry):
        frm = lax.rem(me - d + n, n)
        second(d, frm, frm).wait_recv()
        second(d, lax.rem(me + d, n), me).wait_send()
        first(d, lax.rem(me + d, n)).wait_send()
        return carry

    lax.fori_loop(1, n, end, 0)


def freq_sum(array, collective_id):
    n = array.shape[0]
    block = array.shape[1:]
    dma = pltpu.SemaphoreType.DMA
    return pl.pallas_call(
        functools.partial(freq_sum_kernel, n),
        out_shape=jax.ShapeDtypeStruct(array.shape, array.dtype),
        in_specs=[pl.BlockSpec(memory_space=pltpu.VMEM)],
        out_specs=pl.BlockSpec(memory_space=pltpu.VMEM),
        scratch_shapes=[
            pltpu.VMEM((n,) + block, array.dtype),
            pltpu.VMEM(block, array.dtype),
            dma((n,)),
            dma((n,)),
            dma((n,)),
            dma((n,)),
            dma,
        ],
        compiler_params=pltpu.CompilerParams(
            collective_id=collective_id, has_side_effects=True
        ),
    )(array)


def unit(turns):
    phases = -2.0 * math.pi * turns
    return jnp.cos(phases), jnp.sin(phases)


def dft_tables(pixels):
    cells = np.arange(S) - S // 2
    places = np.arange(pixels) - pixels // 2
    angle = -2.0 * np.pi * np.mod(cells[:, None] * places[None, :], pixels) / pixels
    return np.cos(angle).astype(np.float32), np.sin(angle).astype(np.float32)


def ramp(shift, w_plane, pixels):
    places = jnp.arange(pixels, dtype=jnp.int32) - pixels // 2
    linear = jnp.mod(shift[..., None] * places, pixels).astype(jnp.float32) / pixels
    wrap = 2 * pixels * pixels
    quadratic = jnp.mod(w_plane[..., None] * places * places, wrap).astype(jnp.float32) / wrap
    return linear + quadratic


def kernel_table(position):
    cell_pos = jnp.arange(S, dtype=jnp.float32)
    offset_cells = position[None, :] - cell_pos[:, None]
    values = jnp.exp(offset_cells * offset_cells * (-0.5 / (KERNEL_WIDTH * KERNEL_WIDTH)))
    return values.astype(jnp.bfloat16)


def shards(model, beam, vis_obs, vis_uv, spectral, vis_subgrid, counts, uv_offsets, w_planes):
    rows_own = model.shape[0]
    fs = beam.shape[-1]
    tay = model.shape[1] // fs
    blocks = lax.axis_size("vis")
    groups = lax.axis_size("freq")
    extent = rows_own * blocks
    ns = w_planes.shape[-1]
    nv = vis_obs.shape[-1]
    norm_scale = 1.0 / (S * math.sqrt(groups * blocks * ns))
    rt = tay * rows_own
    bf = jnp.bfloat16
    f32 = jnp.float32

    gain = beam[0].astype(f32)
    model_t = model.reshape(rows_own, tay, fs).transpose(1, 0, 2).astype(f32)
    weighted = (model_t * gain[None]).astype(bf).reshape(rt, fs).astype(f32)

    tile = jnp.concatenate([uv_offsets[0, 0, 1], w_planes[0, 0]]).astype(f32)
    tile = jnp.broadcast_to(jnp.pad(tile, (0, 8 - 2 * ns))[:, None], (8, 128))
    tiles = exchange(tile, "vis", False, 0)
    facts = tiles[:, : 2 * ns, 0].astype(jnp.int32)
    turns = ramp(facts[:, :ns], facts[:, ns:], fs)
    r_re, r_im = unit(turns)

    t_re, t_im = dft_tables(fs)
    t_fwd = np.concatenate(
        [np.concatenate([t_re.T, t_im.T], 1), np.concatenate([-t_im.T, t_re.T], 1)], 0
    )
    t_fwd = jnp.asarray(t_fwd, bf)
    x = jnp.concatenate(
        [weighted * r_re[:, :, None, :], weighted * r_im[:, :, None, :]], axis=-1
    ).astype(bf)
    proj = jnp.dot(x.reshape(blocks * ns * rt, 2 * fs), t_fwd, preferred_element_type=f32)
    proj = proj.reshape(blocks, ns, rt, 2, S).transpose(0, 2, 3, 1, 4)
    proj = proj.reshape(blocks, rt, 2 * ns * S).astype(bf)
    got = exchange(proj, "vis", True, 1)

    l_pix = jnp.arange(extent, dtype=jnp.int32) - extent // 2
    cells = jnp.arange(S, dtype=jnp.int32) - S // 2
    eu = []
    for s in range(ns):
        lin = jnp.mod((uv_offsets[0, 0, 0, s] + cells)[:, None] * l_pix[None, :], extent)
        wrap = 2 * extent * extent
        quad = jnp.mod(w_planes[0, 0, s] * l_pix * l_pix, wrap)
        eu += unit(lin.astype(f32) / extent + (quad.astype(f32) / wrap)[None, :])
    eu = jnp.concatenate(eu, axis=0).astype(bf)

    width = 2 * ns * S
    got = got.reshape(blocks, tay, rows_own, width).transpose(1, 0, 2, 3).reshape(tay, extent, width)
    prod = jnp.einsum("ar,trn->tan", eu, got, preferred_element_type=f32)
    prod = prod.reshape(tay, ns, 2, S, 2, ns, S)
    grid_re = jnp.stack(
        [prod[:, s, 0, :, 0, s] - prod[:, s, 1, :, 1, s] for s in range(ns)], axis=2
    )
    grid_im = jnp.stack(
        [prod[:, s, 0, :, 1, s] + prod[:, s, 1, :, 0, s] for s in range(ns)], axis=2
    )
    grid = jnp.stack([grid_re, grid_im]).astype(bf).reshape(2 * tay * S, ns * S)

    ku = kernel_table(vis_uv[0, 0, 0]).astype(f32)
    kv = kernel_table(vis_uv[0, 0, 1])
    sub = vis_subgrid[0, 0]
    kv = jnp.concatenate([jnp.where(sub[None, :] == s, kv, 0) for s in range(ns)], axis=0).astype(bf)
    spectrum = spectral[0, 0]
    powers = jnp.stack([spectrum**t for t in range(tay)])
    cell = jnp.dot(grid, kv, preferred_element_type=f32).reshape(2, tay, S, nv)
    predicted = jnp.sum(jnp.sum(cell * ku[None, None], axis=2) * powers[None], axis=1)
    live = (jnp.arange(nv, dtype=jnp.int32) < counts[0, 0]).astype(f32)
    residual = live[None] * (vis_obs[0, 0] - predicted)
    spread = ((residual[:, None] * powers[None])[:, :, None] * ku[None, None]).astype(bf)
    rg = lax.dot_general(
        spread.reshape(2 * tay * S, nv), kv, (((1,), (1,)), ((), ())), preferred_element_type=f32
    ).astype(bf)
    rg = rg.reshape(2, tay, S, ns, S)
    zero = jnp.zeros((tay, S, S), bf)
    rows = []
    for s in range(ns):
        re, im = rg[0, :, :, s], rg[1, :, :, s]
        pad = lambda v: [v if k == s else zero for k in range(ns)]
        rows.append(jnp.concatenate(pad(re) + pad(im), axis=-1))
        rows.append(jnp.concatenate(pad(im) + pad(-re), axis=-1))
    rhs = jnp.concatenate(rows, axis=1)
    h = jnp.einsum("ar,tan->trn", eu, rhs, preferred_element_type=f32).astype(bf)
    h = h.reshape(tay, blocks, rows_own, width).transpose(1, 0, 2, 3).reshape(blocks, rt, width)
    back = exchange(h, "vis", True, 2)

    t_bwd = np.zeros((2, ns, S, ns, 2, fs), np.float32)
    for s in range(ns):
        t_bwd[0, s, :, s, 0] = t_re
        t_bwd[1, s, :, s, 0] = t_im
        t_bwd[0, s, :, s, 1] = -t_im
        t_bwd[1, s, :, s, 1] = t_re
    t_bwd = jnp.asarray(t_bwd.reshape(width, ns * 2 * fs), bf)
    z = jnp.dot(back.reshape(blocks * rt, width), t_bwd, preferred_element_type=f32)
    z = z.reshape(blocks, rt, ns, 2, fs)
    term = jnp.sum(
        z[:, :, :, 0] * r_re[:, None] + z[:, :, :, 1] * r_im[:, None], axis=(0, 2)
    )
    image = term.reshape(tay, rows_own, fs) * (gain * norm_scale)[None]
    image = image.transpose(1, 0, 2).reshape(rows_own, groups, tay * fs // groups)
    dirty = freq_sum(image.transpose(1, 0, 2), 3)
    dirty = dirty.transpose(1, 0, 2).reshape(rows_own, tay * fs)
    return (residual.reshape(1, 1, 2, nv), dirty)


def solution(mesh):
    in_specs = (
        P("vis", None),
        P("freq", "vis", None),
        P("freq", "vis", None, None),
        P("freq", "vis", None, None),
        P("freq", "vis", None),
        P("freq", "vis", None),
        P("freq", "vis"),
        P("freq", "vis", None, None),
        P("freq", "vis", None),
    )
    out_specs = (P("freq", "vis", None, None), P("vis", None))
    return jax.shard_map(shards, mesh=mesh, in_specs=in_specs, out_specs=out_specs, check_vma=False)
```

```python
import functools
import math

import jax
import jax.numpy as jnp
import numpy as np
from jax import lax
from jax.experimental import pallas as pl
from jax.experimental.pallas import tpu as pltpu
from jax.sharding import PartitionSpec as P

S = 64
KERNEL_WIDTH = 0.5
MESH = pl.DeviceIdType.MESH
BF = jnp.bfloat16
F32 = jnp.float32
I32 = jnp.int32


def dft_tables(pixels):
    cells = np.arange(S) - S // 2
    places = np.arange(pixels) - pixels // 2
    angle = -2.0 * np.pi * np.mod(cells[:, None] * places[None, :], pixels) / pixels
    return np.cos(angle).astype(np.float32), np.sin(angle).astype(np.float32)


def cos_of(phase, bits):
    full = 1 << bits
    phase = phase & (full - 1)
    phase = jnp.where(phase >= full // 2, full - phase, phase)
    x = (0.25 - phase.astype(F32) * (1.0 / full)) * (2.0 * math.pi)
    y = x * x
    total = jnp.full_like(x, -1.0 / math.factorial(11))
    for power in (9, 7, 5, 3, 1):
        sign = 1.0 if power % 4 == 1 else -1.0
        total = total * y + sign / math.factorial(power)
    return total * x


def phase_of(cell, place, w_plane, log2):
    pixels = 1 << log2
    linear = (cell * place) & (pixels - 1)
    quadratic = (w_plane * place * place) & (2 * pixels * pixels - 1)
    return (linear << (log2 + 1)) + quadratic


def offset(k):
    return ((k + 1) // 2) * (1 - 2 * ((k + 1) % 2))


def whole_kernel(
    dims,
    model_ref, beam_ref, obs_ref, uv_ref, spec_ref, sub_ref, counts_ref, off_ref, w_ref,
    fwd_hbm, bwd_hbm,
    res_ref, dirty_ref,
    t_fwd, t_bwd, mine, facts, ramps, weighted, xbuf, sends, got, stage, eu, eu_t, ku, kv,
    grid, gridded, h, back, image, parts, total,
    tab_sem, fact_s, fact_r, msg_s, msg_r, back_s, back_r, sum_s, sum_r, out_s, out_r,
):
    n, groups, tay, rows, fs, ns, nv = dims
    rt = tay * rows
    extent = n * rows
    log_fs = fs.bit_length() - 1
    log_ext = extent.bit_length() - 1
    lanes = 128
    qs = fs // lanes
    batch = 8
    me = lax.axis_index("vis")
    group = lax.axis_index("freq")
    half = ns * S

    def other(k):
        return lax.rem(me + offset(k) + n, n)

    def remote(src, dst, send, recv, axis, to):
        return pltpu.make_async_remote_copy(
            src_ref=src, dst_ref=dst, send_sem=send, recv_sem=recv,
            device_id={axis: to}, device_id_type=MESH,
        )

    def fact_copy(to, slot):
        return remote(mine, facts.at[slot], fact_s.at[to], fact_r.at[slot], "vis", to)

    def msg_copy(to, slot):
        return remote(sends.at[to], got.at[slot], msg_s.at[to], msg_r.at[slot], "vis", to)

    def back_copy(to, slot):
        return remote(sends.at[to], back.at[slot], back_s.at[to], back_r.at[slot], "vis", to)

    def sum_copy(to, slot):
        return remote(image.at[to], parts.at[slot], sum_s.at[to], sum_r.at[slot], "freq", to)

    width = tay * fs // groups

    def out_copy(to, slot):
        place = dirty_ref.at[:, pl.ds(pl.multiple_of(slot * width, lanes), width)]
        return remote(total, place, out_s.at[to], out_r.at[slot], "freq", to)

    fwd_copy = pltpu.make_async_copy(fwd_hbm, t_fwd, tab_sem.at[0])
    bwd_copy = pltpu.make_async_copy(bwd_hbm, t_bwd, tab_sem.at[1])
    fwd_copy.start()
    bwd_copy.start()
    barrier = pltpu.get_barrier_semaphore()

    def greet(axis, count, index):
        def one(d, carry):
            pl.semaphore_signal(
                barrier, inc=1, device_id={axis: lax.rem(index + d, count)}, device_id_type=MESH
            )
            return carry

        lax.fori_loop(1, count, one, 0)

    greet("vis", n, me)
    greet("freq", groups, group)

    lane = lax.broadcasted_iota(I32, (1, lanes), 1)
    fact = jnp.zeros((1, lanes), F32)
    for s in range(ns):
        fact = jnp.where(lane == s, off_ref[0, 0, 1, s].astype(F32), fact)
        fact = jnp.where(lane == ns + s, w_ref[0, 0, s].astype(F32), fact)
    mine[...] = fact
    gain = beam_ref[0].astype(F32)
    for t in range(tay):
        piece = (model_ref[:, t * fs : (t + 1) * fs].astype(F32) * gain).astype(BF)
        weighted[t * rows : (t + 1) * rows, :] = piece.astype(F32)

    pl.semaphore_wait(barrier, n - 1 + groups - 1)

    def tell(k, carry):
        fact_copy(other(k), me).start()
        return carry

    lax.fori_loop(1, n, tell, 0)
    facts[me] = mine[...]

    shape = (2 * half, extent)
    index = lax.broadcasted_iota(I32, shape, 0)
    place = lax.broadcasted_iota(I32, shape, 1) - extent // 2

    def row_factor(index, place):
        which = index // (2 * S)
        centre = jnp.full_like(index, off_ref[0, 0, 0, 0])
        plane = jnp.full_like(index, w_ref[0, 0, 0])
        for s in range(1, ns):
            centre = jnp.where(which == s, off_ref[0, 0, 0, s], centre)
            plane = jnp.where(which == s, w_ref[0, 0, s], plane)
        cell = centre + (index & (S - 1)) - S // 2
        bits = 2 * log_ext + 1
        quarter = ((index // S) & 1) << (bits - 2)
        return cos_of(phase_of(cell, place, plane, log_ext) + quarter, bits).astype(BF)

    eu[...] = row_factor(index, place)
    shape = (extent, 2 * half)
    eu_t[...] = row_factor(
        lax.broadcasted_iota(I32, shape, 1), lax.broadcasted_iota(I32, shape, 0) - extent // 2
    )

    step = min(512, nv)

    def kernels(i, carry):
        cut = pl.ds(pl.multiple_of(i * step, step), step)
        cells = lax.broadcasted_iota(I32, (S, step), 0).astype(F32)

        def table(position):
            d = position - cells
            return jnp.exp(d * d * (-0.5 / (KERNEL_WIDTH * KERNEL_WIDTH))).astype(BF).astype(F32)

        ku[:, cut] = table(uv_ref[0, 0, 0:1, cut])
        kv_all = table(uv_ref[0, 0, 1:2, cut])
        sub = sub_ref[0, :, cut]
        for s in range(ns):
            kv[s * S : (s + 1) * S, cut] = jnp.where(sub == s, kv_all, 0.0).astype(BF)
        return carry

    lax.fori_loop(0, nv // step, kernels, 0)

    fwd_copy.wait()
    spot = lax.broadcasted_iota(I32, (qs, lanes), 0) * lanes + (
        lax.broadcasted_iota(I32, (qs, lanes), 1) - fs // 2
    )
    low = lax.broadcasted_iota(I32, (rt, half), 1) < S
    bits = 2 * log_fs + 1

    def forward(i, carry):
        for u in range(batch):
            k = i * batch + u
            j = other(k)

            def hear():
                fact_copy(j, j).wait_recv()

            if u == 0:
                pl.when(i > 0)(hear)
            else:
                hear()
            told = facts[j].astype(I32)
            for s in range(ns):
                centre = jnp.broadcast_to(told[:, s : s + 1], (qs, lanes))
                plane = jnp.broadcast_to(told[:, ns + s : ns + s + 1], (qs, lanes))
                phase = phase_of(centre, spot, plane, log_fs)
                top = (u * ns + s) * rt
                for c in range(2):
                    ramp = cos_of(phase + (c << (bits - 2)), bits)
                    ramps[j, s, c] = ramp
                    for q in range(qs):
                        cut = slice(q * lanes, (q + 1) * lanes)
                        at = c * fs + q * lanes
                        xbuf[top : top + rt, at : at + lanes] = (
                            weighted[:, cut] * ramp[q : q + 1, :]
                        ).astype(BF)
        proj = jnp.dot(xbuf[...], t_fwd[...], preferred_element_type=F32)
        for u in range(batch):
            j = other(i * batch + u)
            first = proj[u * ns * rt : u * ns * rt + rt]
            second = proj[u * ns * rt + rt : u * ns * rt + 2 * rt]
            real = jnp.where(low, first, pltpu.roll(second, S, 1))
            imag = jnp.where(low, pltpu.roll(first, S, 1), second)
            sends[j, :, :half] = real.astype(BF)
            sends[j, :, half:] = imag.astype(BF)

            def go():
                msg_copy(j, me).start()

            if u == 0:
                pl.when(i > 0)(go)
            else:
                go()
        return carry

    lax.fori_loop(0, n // batch, forward, 0)
    got[me] = sends[me]

    def arrive(k, carry):
        j = other(k)
        msg_copy(j, j).wait_recv()
        return carry

    lax.fori_loop(1, n, arrive, 0)

    for p in range(n // 2):
        one = got[2 * p].astype(F32)
        two = got[2 * p + 1].astype(F32)
        for t in range(tay):
            cut = slice(t * rows, (t + 1) * rows)
            both = jnp.concatenate([one[cut], two[cut]], axis=0).astype(BF)
            stage[t, 2 * rows * p : 2 * rows * (p + 1), :] = both
    first_sub = lax.broadcasted_iota(I32, (S, half), 1) < S
    for t in range(tay):
        prod = jnp.dot(eu[...], stage[t], preferred_element_type=F32)
        re, im = [], []
        for s in range(ns):
            top = prod[2 * s * S : (2 * s + 1) * S]
            bot = prod[(2 * s + 1) * S : (2 * s + 2) * S]
            re.append(top[:, :half] - bot[:, half:])
            im.append(top[:, half:] + bot[:, :half])
        grid[2 * t * S : (2 * t + 1) * S, :] = jnp.where(first_sub, re[0], re[1]).astype(BF)
        grid[(2 * t + 1) * S : (2 * t + 2) * S, :] = jnp.where(first_sub, im[0], im[1]).astype(BF)

    gridded[...] = jnp.zeros_like(gridded)

    def visit(i, carry):
        cut = pl.ds(pl.multiple_of(i * step, step), step)
        ku_cut = ku[:, cut]
        kv_cut = kv[:, cut]
        spec = spec_ref[0, :, cut]
        powers = [jnp.ones_like(spec)]
        for t in range(1, tay):
            powers.append(powers[-1] * spec)
        cell = jnp.dot(grid[...], kv_cut, preferred_element_type=F32)
        number = lax.broadcasted_iota(I32, (1, step), 1) + i * step
        live = (number < counts_ref[0, 0]).astype(F32)
        spread = []
        left = []
        for c in range(2):
            predicted = jnp.zeros((1, step), F32)
            for t in range(tay):
                top = (2 * t + c) * S
                part = jnp.sum(cell[top : top + S] * ku_cut, axis=0, keepdims=True)
                predicted = predicted + part * powers[t]
            left.append(live * (obs_ref[0, 0, c : c + 1, cut] - predicted))
            res_ref[0, 0, c : c + 1, cut] = left[c]
        for t in range(tay):
            for c in range(2):
                spread.append(((left[c] * powers[t]) * ku_cut).astype(BF))
        spread = jnp.concatenate(spread, axis=0)
        gridded[...] += lax.dot_general(
            spread, kv_cut, (((1,), (1,)), ((), ())), preferred_element_type=F32
        )
        return carry

    lax.fori_loop(0, nv // step, visit, 0)

    def sent(k, carry):
        msg_copy(other(k), me).wait_send()
        return carry

    lax.fori_loop(1, n, sent, 0)
    for t in range(tay):
        re = gridded[2 * t * S : (2 * t + 1) * S, :].astype(BF).astype(F32)
        im = gridded[(2 * t + 1) * S : (2 * t + 2) * S, :].astype(BF).astype(F32)
        rhs = []
        for s in range(ns):
            keep = first_sub if s == 0 else jnp.logical_not(first_sub)
            re_s = jnp.where(keep, re, 0.0)
            im_s = jnp.where(keep, im, 0.0)
            rhs.append(jnp.concatenate([re_s, im_s], axis=1))
            rhs.append(jnp.concatenate([im_s, -re_s], axis=1))
        rhs = jnp.concatenate(rhs, axis=0).astype(BF)
        h[t] = jnp.dot(eu_t[...], rhs, preferred_element_type=F32)
    for j in range(n):
        sends[j] = jnp.concatenate(
            [h[t, j * rows : (j + 1) * rows, :] for t in range(tay)], axis=0
        ).astype(BF)

    def give(k, carry):
        back_copy(other(k), me).start()
        return carry

    lax.fori_loop(1, n, give, 0)
    back[me] = sends[me]
    bwd_copy.wait()

    weighted[...] = jnp.zeros_like(weighted)

    def collect(i, carry):
        for u in range(batch):
            j = other(i * batch + u)

            def hear():
                back_copy(j, j).wait_recv()

            if u == 0:
                pl.when(i > 0)(hear)
            else:
                hear()
        lhs = jnp.concatenate([back[other(i * batch + u)] for u in range(batch)], axis=0)

        def columns(q, carry):
            wide = 2 * ns * lanes
            z = jnp.dot(lhs, t_bwd[q], preferred_element_type=F32)
            at = pl.ds(pl.multiple_of(q * lanes, lanes), lanes)
            acc = weighted[:, at]
            for u in range(batch):
                j = other(i * batch + u)
                for s in range(ns):
                    for c in range(2):
                        v = (s * 2 + c) * lanes
                        ramp = ramps[j, s, c, pl.ds(q, 1), :]
                        acc = acc + z[u * rt : (u + 1) * rt, v : v + lanes] * ramp
            weighted[:, at] = acc
            return carry

        lax.fori_loop(0, qs, columns, 0)
        return carry

    lax.fori_loop(0, n // batch, collect, 0)

    norm_scale = 1.0 / (S * math.sqrt(groups * n * ns))
    scaled = gain * norm_scale
    per = groups // tay
    for f in range(groups):
        t = f // per
        cut = slice((f % per) * width, (f % per + 1) * width)
        image[f] = weighted[t * rows : (t + 1) * rows, cut] * scaled[:, cut]

    def peer(d):
        return lax.rem(group + d, groups)

    def share(d, carry):
        sum_copy(peer(d), group).start()
        return carry

    lax.fori_loop(1, groups, share, 0)
    total[...] = image[group]

    def add(d, carry):
        j = peer(d)
        sum_copy(j, j).wait_recv()
        total[...] += parts[j]
        return carry

    lax.fori_loop(1, groups, add, 0)

    def publish(d, carry):
        out_copy(peer(d), group).start()
        return carry

    lax.fori_loop(1, groups, publish, 0)
    dirty_ref[:, pl.ds(pl.multiple_of(group * width, lanes), width)] = total[...]

    def finish(k, carry):
        to = other(k)
        fact_copy(to, me).wait_send()
        back_copy(to, me).wait_send()
        return carry

    lax.fori_loop(1, n, finish, 0)

    def close(d, carry):
        j = peer(d)
        sum_copy(j, group).wait_send()
        out_copy(j, group).wait_send()
        out_copy(j, j).wait_recv()
        return carry

    lax.fori_loop(1, groups, close, 0)


def shards(model, beam, vis_obs, vis_uv, spectral, vis_subgrid, counts, uv_offsets, w_planes):
    rows = model.shape[0]
    fs = beam.shape[-1]
    tay = model.shape[1] // fs
    n = lax.axis_size("vis")
    groups = lax.axis_size("freq")
    extent = rows * n
    ns = w_planes.shape[-1]
    nv = vis_obs.shape[-1]
    rt = tay * rows
    width = 2 * ns * S
    lanes = 128
    qs = fs // lanes

    t_re, t_im = dft_tables(fs)
    fwd = np.concatenate(
        [np.concatenate([t_re.T, t_im.T], 1), np.concatenate([-t_im.T, t_re.T], 1)], 0
    )
    bwd = np.zeros((2, ns, S, qs, ns, 2, lanes), np.float32)
    for s in range(ns):
        split = (S, qs, lanes)
        bwd[0, s, :, :, s, 0] = t_re.reshape(split)
        bwd[1, s, :, :, s, 0] = t_im.reshape(split)
        bwd[0, s, :, :, s, 1] = -t_im.reshape(split)
        bwd[1, s, :, :, s, 1] = t_re.reshape(split)
    bwd = bwd.reshape(width, qs, ns * 2 * lanes).transpose(1, 0, 2)

    dma = pltpu.SemaphoreType.DMA
    vmem = pl.BlockSpec(memory_space=pltpu.VMEM)
    smem = pl.BlockSpec(memory_space=pltpu.SMEM)
    hbm = pl.BlockSpec(memory_space=pl.ANY)
    dims = (n, groups, tay, rows, fs, ns, nv)
    return pl.pallas_call(
        functools.partial(whole_kernel, dims),
        name="whole",
        out_shape=(
            jax.ShapeDtypeStruct((1, 1, 2, nv), F32),
            jax.ShapeDtypeStruct((rows, tay * fs), F32),
        ),
        in_specs=[vmem] * 6 + [smem] * 3 + [hbm] * 2,
        out_specs=(vmem, vmem),
        scratch_shapes=[
            pltpu.VMEM((2 * fs, 2 * S), BF),
            pltpu.VMEM((qs, width, ns * 2 * lanes), BF),
            pltpu.VMEM((1, lanes), F32),
            pltpu.VMEM((n, 1, lanes), F32),
            pltpu.VMEM((n, ns, 2, qs, lanes), F32),
            pltpu.VMEM((rt, fs), F32),
            pltpu.VMEM((8 * ns * rt, 2 * fs), BF),
            pltpu.VMEM((n, rt, width), BF),
            pltpu.VMEM((n, rt, width), BF),
            pltpu.VMEM((tay, extent, width), BF),
            pltpu.VMEM((width, extent), BF),
            pltpu.VMEM((extent, width), BF),
            pltpu.VMEM((S, nv), F32),
            pltpu.VMEM((ns * S, nv), BF),
            pltpu.VMEM((2 * tay * S, ns * S), BF),
            pltpu.VMEM((2 * tay * S, ns * S), F32),
            pltpu.VMEM((tay, extent, width), F32),
            pltpu.VMEM((n, rt, width), BF),
            pltpu.VMEM((groups, rows, tay * fs // groups), F32),
            pltpu.VMEM((groups, rows, tay * fs // groups), F32),
            pltpu.VMEM((rows, tay * fs // groups), F32),
            dma((2,)),
            dma((n,)), dma((n,)),
            dma((n,)), dma((n,)),
            dma((n,)), dma((n,)),
            dma((groups,)), dma((groups,)),
            dma((groups,)), dma((groups,)),
        ],
        compiler_params=pltpu.CompilerParams(
            collective_id=0, has_side_effects=True, vmem_limit_bytes=48 * 2**20
        ),
    )(
        model, beam, vis_obs, vis_uv, spectral, vis_subgrid, counts, uv_offsets, w_planes,
        jnp.asarray(fwd, BF), jnp.asarray(bwd, BF),
    )


def solution(mesh):
    in_specs = (
        P("vis", None),
        P("freq", "vis", None),
        P("freq", "vis", None, None),
        P("freq", "vis", None, None),
        P("freq", "vis", None),
        P("freq", "vis", None),
        P("freq", "vis"),
        P("freq", "vis", None, None),
        P("freq", "vis", None),
    )
    out_specs = (P("freq", "vis", None, None), P("vis", None))
    return jax.shard_map(shards, mesh=mesh, in_specs=in_specs, out_specs=out_specs, check_vma=False)
```

```python
import functools
import math

import jax
import jax.numpy as jnp
import numpy as np
from jax import lax
from jax.experimental import pallas as pl
from jax.experimental.pallas import tpu as pltpu
from jax.sharding import PartitionSpec as P

S = 64
KERNEL_WIDTH = 0.5
MESH = pl.DeviceIdType.MESH
BF = jnp.bfloat16
F32 = jnp.float32
I32 = jnp.int32


def dft_tables(pixels):
    cells = np.arange(S) - S // 2
    places = np.arange(pixels) - pixels // 2
    angle = -2.0 * np.pi * np.mod(cells[:, None] * places[None, :], pixels) / pixels
    return np.cos(angle).astype(np.float32), np.sin(angle).astype(np.float32)


def cos_of(phase, bits):
    full = 1 << bits
    phase = phase & (full - 1)
    phase = jnp.where(phase >= full // 2, full - phase, phase)
    x = (0.25 - phase.astype(F32) * (1.0 / full)) * (2.0 * math.pi)
    y = x * x
    total = jnp.full_like(x, -1.0 / math.factorial(11))
    for power in (9, 7, 5, 3, 1):
        sign = 1.0 if power % 4 == 1 else -1.0
        total = total * y + sign / math.factorial(power)
    return total * x


def phase_of(cell, place, w_plane, log2):
    pixels = 1 << log2
    linear = (cell * place) & (pixels - 1)
    quadratic = (w_plane * place * place) & (2 * pixels * pixels - 1)
    return (linear << (log2 + 1)) + quadratic


def offset(k):
    return ((k + 1) // 2) * (1 - 2 * ((k + 1) % 2))


def whole_kernel(
    dims,
    model_hbm, beam_hbm, obs_hbm, uv_hbm, spec_hbm, sub_hbm, counts_hbm, off_hbm, w_hbm,
    fwd_hbm, bwd_hbm,
    res_ref, dirty_ref,
    model_ref, beam_ref, obs_ref, uv_ref, spec_ref, sub_ref, counts_ref, off_ref, w_ref,
    t_fwd, t_bwd, mine, facts, ramps, packed, far_packed, beams, far_beams, weighted,
    xbuf, sends, got, stage, eu, eu_t, ku, kv, grid, gridded, h, back_sends, back, image, parts,
    total, far_total,
    tab_sem, fact_s, fact_r, pair_s, pair_r, msg_s, msg_r, back_s, back_r, sum_s, sum_r,
    out_s, out_r,
):
    n, groups, tay, rows, fs, ns, nv = dims
    rt = tay * rows
    extent = n * rows
    log_fs = fs.bit_length() - 1
    log_ext = extent.bit_length() - 1
    lanes = 128
    wide = 2 * S
    qs = fs // lanes
    batch = 8
    me = lax.axis_index("vis")
    group = lax.axis_index("freq")

    near = n // 2
    twin = lax.rem(me + near, n)

    def other(k):
        return lax.rem(me + offset(k) + n, n)

    def actor(k):
        return lax.rem(me - offset(k) + n, n)

    def twin_of(device):
        return lax.rem(device + near, n)

    def remote(src, dst, send, recv, axis, to):
        return pltpu.make_async_remote_copy(
            src_ref=src, dst_ref=dst, send_sem=send, recv_sem=recv,
            device_id={axis: to}, device_id_type=MESH,
        )

    def fact_copy(to, slot):
        return remote(mine, facts.at[slot], fact_s.at[to], fact_r.at[slot], "vis", to)

    def pair_copy(src, dst, index):
        return remote(src, dst, pair_s.at[index], pair_r.at[index], "vis", twin)

    def msg_copy(s, r, to, slot):
        return remote(
            sends.at[s, r, to], got.at[s, slot], msg_s.at[s, r, to], msg_r.at[s, slot], "vis", to
        )

    def back_copy(s, r, to, rows_of, slot):
        return remote(
            back_sends.at[s, rows_of], back.at[s, r, slot],
            back_s.at[s, rows_of], back_r.at[s, r, slot], "vis", to,
        )

    def sum_copy(r, to, slot):
        return remote(
            image.at[r, to], parts.at[r, slot], sum_s.at[r, to], sum_r.at[r, slot], "freq", to
        )

    width = tay * fs // groups

    def out_copy(to, slot):
        place = dirty_ref.at[:, pl.ds(pl.multiple_of(slot * width, lanes), width)]
        return remote(total.at[0], place, out_s.at[to], out_r.at[slot], "freq", to)

    loads = [
        (off_hbm, off_ref),
        (w_hbm, w_ref),
        (beam_hbm, beam_ref),
        (model_hbm, model_ref),
        (uv_hbm, uv_ref),
        (sub_hbm, sub_ref),
        (fwd_hbm, t_fwd),
        (counts_hbm, counts_ref),
        (spec_hbm, spec_ref),
        (obs_hbm, obs_ref),
        (bwd_hbm, t_bwd),
    ]
    loads = [pltpu.make_async_copy(a, b, tab_sem.at[i]) for i, (a, b) in enumerate(loads)]
    for load in loads:
        load.start()
    barrier = pltpu.get_barrier_semaphore()

    def greet(axis, to):
        pl.semaphore_signal(barrier, inc=1, device_id={axis: to}, device_id_type=MESH)

    greet("vis", twin)
    greet("vis", actor(near - 1))

    def greet_near(k, carry):
        greet("vis", other(near - k))
        return carry

    def greet_group(d, carry):
        greet("freq", lax.rem(group + d, groups))
        return carry

    lax.fori_loop(1, near, greet_near, 0)
    lax.fori_loop(1, groups, greet_group, 0)

    for load in loads[:4]:
        load.wait()
    lane = lax.broadcasted_iota(I32, (1, lanes), 1)
    fact = jnp.zeros((1, lanes), F32)
    for s in range(ns):
        fact = jnp.where(lane == s, off_ref[0, 0, 1, s].astype(F32), fact)
        fact = jnp.where(lane == ns + s, w_ref[0, 0, s].astype(F32), fact)
    mine[...] = fact
    gain = beam_ref[0].astype(F32)
    for t in range(tay):
        piece = (model_ref[:, t * fs : (t + 1) * fs].astype(F32) * gain).astype(BF)
        weighted[0, t * rows : (t + 1) * rows, :] = piece.astype(F32)
    packed[...] = weighted[0].astype(BF)
    beams[...] = jnp.concatenate([gain[:, : fs // 2], gain[:, fs // 2 :]], axis=0).astype(BF)

    pl.semaphore_wait(barrier, near + 1 + groups - 1)
    pair_copy(packed, far_packed, 0).start()

    def tell(k, carry):
        fact_copy(actor(k), me).start()
        return carry

    lax.fori_loop(1, near, tell, 0)
    pair_copy(beams, far_beams, 1).start()
    facts[me] = mine[...]

    loads[6].wait()
    spot = lax.broadcasted_iota(I32, (qs, lanes), 0) * lanes + (
        lax.broadcasted_iota(I32, (qs, lanes), 1) - fs // 2
    )
    bits = 2 * log_fs + 1

    def forward(r, s, i, carry):
        for u in range(batch):
            j = other(i * batch + u)

            def hear():
                fact_copy(j, j).wait_recv()

            if r == 0 and s == 0:
                if u == 0:
                    pl.when(i > 0)(hear)
                else:
                    hear()
            if r == 0:
                told = facts[j].astype(I32)
                centre = jnp.broadcast_to(told[:, s : s + 1], (qs, lanes))
                plane = jnp.broadcast_to(told[:, ns + s : ns + s + 1], (qs, lanes))
                phase = phase_of(centre, spot, plane, log_fs)
                for c in range(2):
                    ramps[j, s, c] = cos_of(phase + (c << (bits - 2)), bits)
            for c in range(2):
                ramp = ramps[j, s, c]
                for q in range(qs):
                    cut = slice(q * lanes, (q + 1) * lanes)
                    at = c * fs + q * lanes
                    xbuf[u * rt : (u + 1) * rt, at : at + lanes] = (
                        weighted[r, :, cut] * ramp[q : q + 1, :]
                    ).astype(BF)
        proj = jnp.dot(xbuf[...], t_fwd[...], preferred_element_type=F32).astype(BF)
        for u in range(batch):
            j = other(i * batch + u)
            sends[s, r, j] = proj[u * rt : (u + 1) * rt]

            def go():
                msg_copy(s, r, j, me if r == 0 else twin).start()

            if u == 0:
                pl.when(i > 0)(go)
            else:
                go()
        return carry

    for r in range(2):
        if r == 1:
            pair_copy(packed, far_packed, 0).wait_recv()
            weighted[1] = far_packed[...].astype(F32)
        for s in range(ns):
            lax.fori_loop(0, near // batch, functools.partial(forward, r, s), 0)
            got[s, me if r == 0 else twin] = sends[s, r, me]
        if r == 0:
            def row_factor(s, index, place):
                cell = off_ref[0, 0, 0, s] + (index & (S - 1)) - S // 2
                bits = 2 * log_ext + 1
                quarter = (index // S) << (bits - 2)
                return cos_of(phase_of(cell, place, w_ref[0, 0, s], log_ext) + quarter, bits).astype(BF)

            def place_of(shape, axis):
                return lax.broadcasted_iota(I32, shape, axis) - extent // 2

            shape = (wide, extent)
            turned = (extent, wide)
            for s in range(ns):
                eu[s] = row_factor(s, lax.broadcasted_iota(I32, shape, 0), place_of(shape, 1))
                eu_t[s] = row_factor(s, lax.broadcasted_iota(I32, turned, 1), place_of(turned, 0))

            loads[4].wait()
            loads[5].wait()
            step = min(512, nv)

            def kernels(i, carry):
                cut = pl.ds(pl.multiple_of(i * step, step), step)
                cells = lax.broadcasted_iota(I32, (S, step), 0).astype(F32)

                def table(position):
                    d = position - cells
                    return jnp.exp(d * d * (-0.5 / (KERNEL_WIDTH * KERNEL_WIDTH))).astype(BF).astype(F32)

                ku[:, cut] = table(uv_ref[0, 0, 0:1, cut])
                kv_all = table(uv_ref[0, 0, 1:2, cut])
                sub = sub_ref[0, :, cut]
                for s in range(ns):
                    masked = jnp.where(sub == s, kv_all, 0.0).astype(BF)
                    kv[s, :S, cut] = masked
                    kv[s, S:, cut] = masked
                return carry

            lax.fori_loop(0, nv // step, kernels, 0)

    for load in loads[7:10]:
        load.wait()
    first = lax.broadcasted_iota(I32, (S, wide), 1) < S
    sign = jnp.where(first, -1.0, 1.0)

    for s in range(ns):

        def arrive(k, carry):
            j = actor(k)
            msg_copy(s, 0, j, j).wait_recv()
            msg_copy(s, 1, j, twin_of(j)).wait_recv()
            return carry

        lax.fori_loop(1, near, arrive, 0)

        for p in range(n // 2):
            one = got[s, 2 * p].astype(F32)
            two = got[s, 2 * p + 1].astype(F32)
            for t in range(tay):
                cut = slice(t * rows, (t + 1) * rows)
                both = jnp.concatenate([one[cut], two[cut]], axis=0).astype(BF)
                stage[t, 2 * rows * p : 2 * rows * (p + 1), :] = both
        for t in range(tay):
            prod = jnp.dot(eu[s], stage[t], preferred_element_type=F32)
            pair = prod[:S] + sign * pltpu.roll(prod[S:], S, 1)
            grid[2 * t * S : (2 * t + 1) * S, :] = jnp.where(first, pair, 0.0).astype(BF)
            grid[(2 * t + 1) * S : (2 * t + 2) * S, :] = jnp.where(first, 0.0, pair).astype(BF)

        gridded[...] = jnp.zeros_like(gridded)

        def visit(i, carry):
            cut = pl.ds(pl.multiple_of(i * step, step), step)
            ku_cut = ku[:, cut]
            kv_cut = kv[s, :, cut]
            spec = spec_ref[0, :, cut]
            powers = [jnp.ones_like(spec)]
            for t in range(1, tay):
                powers.append(powers[-1] * spec)
            cell = jnp.dot(grid[...], kv_cut, preferred_element_type=F32)
            number = lax.broadcasted_iota(I32, (1, step), 1) + i * step
            live = jnp.logical_and(number < counts_ref[0, 0], sub_ref[0, :, cut] == s)
            live = live.astype(F32)
            spread = []
            left = []
            for c in range(2):
                predicted = jnp.zeros((1, step), F32)
                for t in range(tay):
                    top = (2 * t + c) * S
                    part = jnp.sum(cell[top : top + S] * ku_cut, axis=0, keepdims=True)
                    predicted = predicted + part * powers[t]
                left.append(live * (obs_ref[0, 0, c : c + 1, cut] - predicted))
                if s == 0:
                    res_ref[0, 0, c : c + 1, cut] = left[c]
                else:
                    res_ref[0, 0, c : c + 1, cut] += left[c]
            for t in range(tay):
                for c in range(2):
                    spread.append(((left[c] * powers[t]) * ku_cut).astype(BF))
            spread = jnp.concatenate(spread, axis=0)
            gridded[...] += lax.dot_general(
                spread, kv_cut, (((1,), (1,)), ((), ())), preferred_element_type=F32
            )
            return carry

        lax.fori_loop(0, nv // step, visit, 0)

        for t in range(tay):
            re = gridded[2 * t * S : (2 * t + 1) * S, :]
            im = gridded[(2 * t + 1) * S : (2 * t + 2) * S, :]
            rhs = jnp.concatenate([jnp.where(first, re, im), jnp.where(first, im, -re)], axis=0)
            h[t] = jnp.dot(eu_t[s], rhs.astype(BF), preferred_element_type=F32)
        for j in range(n):
            back_sends[s, j] = jnp.concatenate(
                [h[t, j * rows : (j + 1) * rows, :] for t in range(tay)], axis=0
            ).astype(BF)

        for r in (1, 0):

            def give(k, carry):
                to = actor(k)
                back_copy(s, r, to, to if r == 0 else twin_of(to), me).start()
                return carry

            lax.fori_loop(1, near, give, 0)
        back[s, 0, me] = back_sends[s, me]
        back[s, 1, me] = back_sends[s, twin]

    loads[10].wait()
    weighted[...] = jnp.zeros_like(weighted)
    norm_scale = 1.0 / (S * math.sqrt(groups * n * ns))
    per = groups // tay
    pair_copy(beams, far_beams, 1).wait_recv()
    far_gain = far_beams[...].astype(F32)
    far_gain = jnp.concatenate([far_gain[:rows], far_gain[rows:]], axis=1)

    def peer(d):
        return lax.rem(group + d, groups)

    for s in range(ns):
        for r in (1, 0):

            def collect(i, carry):
                blocks = [other(i * batch + u) for u in range(batch)]
                for u, j in enumerate(blocks):

                    def hear():
                        back_copy(s, r, j, j, j).wait_recv()

                    if u == 0:
                        pl.when(i > 0)(hear)
                    else:
                        hear()
                lhs = jnp.concatenate([back[s, r, j] for j in blocks], axis=0)
                for q in range(qs):
                    z = jnp.dot(lhs, t_bwd[q], preferred_element_type=F32)
                    cut = slice(q * lanes, (q + 1) * lanes)
                    acc = weighted[r, :, cut]
                    for u, j in enumerate(blocks):
                        for c in range(2):
                            ramp = ramps[j, s, c, q : q + 1, :]
                            part = z[u * rt : (u + 1) * rt, c * lanes : (c + 1) * lanes]
                            acc = acc + part * ramp
                    weighted[r, :, cut] = acc
                return carry

            lax.fori_loop(0, near // batch, collect, 0)
            if s == ns - 1:
                scaled = (gain if r == 0 else far_gain) * norm_scale
                for f in range(groups):
                    t = f // per
                    cut = slice((f % per) * width, (f % per + 1) * width)
                    image[r, f] = weighted[r, t * rows : (t + 1) * rows, cut] * scaled[:, cut]

                def share(d, carry):
                    sum_copy(r, peer(d), group).start()
                    return carry

                lax.fori_loop(1, groups, share, 0)

    for r in (1, 0):
        total[r] = image[r, group]

        def add(d, carry):
            j = peer(d)
            sum_copy(r, j, j).wait_recv()
            total[r] += parts[r, j]
            return carry

        lax.fori_loop(1, groups, add, 0)
        if r == 1:
            pair_copy(total.at[1], far_total, 2).start()
    pair_copy(total.at[1], far_total, 2).wait_recv()
    total[0] += far_total[...]

    def publish(d, carry):
        out_copy(peer(d), group).start()
        return carry

    lax.fori_loop(1, groups, publish, 0)
    dirty_ref[:, pl.ds(pl.multiple_of(group * width, lanes), width)] = total[0]

    pair_copy(packed, far_packed, 0).wait_send()
    pair_copy(beams, far_beams, 1).wait_send()
    pair_copy(total.at[1], far_total, 2).wait_send()

    def finish(k, carry):
        to = other(k)
        of = actor(k)
        fact_copy(of, me).wait_send()
        for s in range(ns):
            for r in range(2):
                msg_copy(s, r, to, me).wait_send()
                back_copy(s, r, of, of if r == 0 else twin_of(of), me).wait_send()
        return carry

    lax.fori_loop(1, near, finish, 0)

    def close(d, carry):
        j = peer(d)
        for r in range(2):
            sum_copy(r, j, group).wait_send()
        out_copy(j, group).wait_send()
        out_copy(j, j).wait_recv()
        return carry

    lax.fori_loop(1, groups, close, 0)


def shards(model, beam, vis_obs, vis_uv, spectral, vis_subgrid, counts, uv_offsets, w_planes):
    rows = model.shape[0]
    fs = beam.shape[-1]
    tay = model.shape[1] // fs
    n = lax.axis_size("vis")
    groups = lax.axis_size("freq")
    extent = rows * n
    ns = w_planes.shape[-1]
    nv = vis_obs.shape[-1]
    rt = tay * rows
    wide = 2 * S
    lanes = 128
    qs = fs // lanes

    t_re, t_im = dft_tables(fs)
    fwd = np.concatenate(
        [np.concatenate([t_re.T, t_im.T], 1), np.concatenate([-t_im.T, t_re.T], 1)], 0
    )
    split = (S, qs, 1, lanes)
    re, im = t_re.reshape(split), t_im.reshape(split)
    bwd = np.concatenate(
        [np.concatenate([re, -im], 2), np.concatenate([im, re], 2)], 0
    )
    bwd = bwd.reshape(2 * S, qs, 2 * lanes).transpose(1, 0, 2)

    dma = pltpu.SemaphoreType.DMA
    vmem = pl.BlockSpec(memory_space=pltpu.VMEM)
    hbm = pl.BlockSpec(memory_space=pltpu.HBM)
    dims = (n, groups, tay, rows, fs, ns, nv)
    return pl.pallas_call(
        functools.partial(whole_kernel, dims),
        name="whole",
        out_shape=(
            jax.ShapeDtypeStruct((1, 1, 2, nv), F32),
            jax.ShapeDtypeStruct((rows, tay * fs), F32),
        ),
        in_specs=[hbm] * 11,
        out_specs=(vmem, vmem),
        scratch_shapes=[
            pltpu.VMEM((rows, tay * fs), BF),
            pltpu.VMEM((1, rows, fs), BF),
            pltpu.VMEM((1, 1, 2, nv), F32),
            pltpu.VMEM((1, 1, 2, nv), F32),
            pltpu.VMEM((1, 1, nv), F32),
            pltpu.VMEM((1, 1, nv), I32),
            pltpu.SMEM((1, 1), I32),
            pltpu.SMEM((1, 1, 2, ns), I32),
            pltpu.SMEM((1, 1, ns), I32),
            pltpu.VMEM((2 * fs, wide), BF),
            pltpu.VMEM((qs, wide, 2 * lanes), BF),
            pltpu.VMEM((1, lanes), F32),
            pltpu.VMEM((n, 1, lanes), F32),
            pltpu.VMEM((n, ns, 2, qs, lanes), F32),
            pltpu.VMEM((rt, fs), BF),
            pltpu.VMEM((rt, fs), BF),
            pltpu.VMEM((2 * rows, fs // 2), BF),
            pltpu.VMEM((2 * rows, fs // 2), BF),
            pltpu.VMEM((2, rt, fs), F32),
            pltpu.VMEM((8 * rt, 2 * fs), BF),
            pltpu.VMEM((ns, 2, n, rt, wide), BF),
            pltpu.VMEM((ns, n, rt, wide), BF),
            pltpu.VMEM((tay, extent, wide), BF),
            pltpu.VMEM((ns, wide, extent), BF),
            pltpu.VMEM((ns, extent, wide), BF),
            pltpu.VMEM((S, nv), F32),
            pltpu.VMEM((ns, wide, nv), BF),
            pltpu.VMEM((2 * tay * S, wide), BF),
            pltpu.VMEM((2 * tay * S, wide), F32),
            pltpu.VMEM((tay, extent, wide), F32),
            pltpu.VMEM((ns, n, rt, wide), BF),
            pltpu.VMEM((ns, 2, n, rt, wide), BF),
            pltpu.VMEM((2, groups, rows, tay * fs // groups), F32),
            pltpu.VMEM((2, groups, rows, tay * fs // groups), F32),
            pltpu.VMEM((2, rows, tay * fs // groups), F32),
            pltpu.VMEM((rows, tay * fs // groups), F32),
            dma((11,)),
            dma((n,)), dma((n,)),
            dma((3,)), dma((3,)),
            dma((ns, 2, n)), dma((ns, n)),
            dma((ns, n)), dma((ns, 2, n)),
            dma((2, groups)), dma((2, groups)),
            dma((groups,)), dma((groups,)),
        ],
        compiler_params=pltpu.CompilerParams(
            collective_id=0, has_side_effects=True, vmem_limit_bytes=60 * 2**20
        ),
    )(
        model, beam, vis_obs, vis_uv, spectral, vis_subgrid, counts, uv_offsets, w_planes,
        np.ascontiguousarray(fwd).astype(BF), np.ascontiguousarray(bwd).astype(BF),
    )


def solution(mesh):
    in_specs = (
        P("vis", None),
        P("freq", "vis", None),
        P("freq", "vis", None, None),
        P("freq", "vis", None, None),
        P("freq", "vis", None),
        P("freq", "vis", None),
        P("freq", "vis"),
        P("freq", "vis", None, None),
        P("freq", "vis", None),
    )
    out_specs = (P("freq", "vis", None, None), P("vis", None))
    return jax.shard_map(shards, mesh=mesh, in_specs=in_specs, out_specs=out_specs, check_vma=False)
```

```python
import functools
import math

import jax
import jax.numpy as jnp
import numpy as np
from jax import lax
from jax.experimental import pallas as pl
from jax.experimental.pallas import tpu as pltpu
from jax.sharding import PartitionSpec as P

S = 64
KERNEL_WIDTH = 0.5
MESH = pl.DeviceIdType.MESH
BF = jnp.bfloat16
F32 = jnp.float32
I32 = jnp.int32


def dft_tables(pixels):
    cells = np.arange(S) - S // 2
    places = np.arange(pixels) - pixels // 2
    angle = -2.0 * np.pi * np.mod(cells[:, None] * places[None, :], pixels) / pixels
    return np.cos(angle).astype(np.float32), np.sin(angle).astype(np.float32)


def cos_of(phase, bits):
    full = 1 << bits
    phase = phase & (full - 1)
    phase = jnp.where(phase >= full // 2, full - phase, phase)
    x = (0.25 - phase.astype(F32) * (1.0 / full)) * (2.0 * math.pi)
    y = x * x
    total = jnp.full_like(x, -1.0 / math.factorial(11))
    for power in (9, 7, 5, 3, 1):
        sign = 1.0 if power % 4 == 1 else -1.0
        total = total * y + sign / math.factorial(power)
    return total * x


def phase_of(cell, place, w_plane, log2):
    pixels = 1 << log2
    linear = (cell * place) & (pixels - 1)
    quadratic = (w_plane * place * place) & (2 * pixels * pixels - 1)
    return (linear << (log2 + 1)) + quadratic


def offset(k):
    return ((k + 1) // 2) * (1 - 2 * ((k + 1) % 2))


def whole_kernel(
    dims,
    model_hbm, beam_hbm, obs_hbm, uv_hbm, spec_hbm, sub_hbm, counts_hbm, off_hbm, w_hbm,
    fwd_hbm, bwd_hbm,
    res_ref, dirty_ref,
    model_ref, beam_ref, obs_ref, uv_ref, spec_ref, sub_ref, counts_ref, off_ref, w_ref,
    t_fwd, t_bwd, mine, facts, ramps, hold, beams, weighted,
    xbuf, sends, got, stage, eu, eu_t, ku, kv, grid, gridded, h, back_sends, back, image, parts,
    stage_f32, total, homes, result,
    tab_sem, fact_s, fact_r, pair_s, pair_r, beam_s, beam_r, home_s, home_r,
    msg_s, msg_r, back_s, back_r, sum_s, sum_r, out_s, out_r,
):
    n, groups, tay, rows, fs, ns, nv = dims
    rt = tay * rows
    extent = n * rows
    log_fs = fs.bit_length() - 1
    log_ext = extent.bit_length() - 1
    lanes = 128
    wide = 2 * S
    qs = fs // lanes
    me = lax.axis_index("vis")
    group = lax.axis_index("freq")

    sets = 4
    close = n // sets

    def other(k):
        return lax.rem(me + offset(k) + n, n)

    def actor(k):
        return lax.rem(me - offset(k) + n, n)

    def owner(device, e):
        return lax.rem(device + e * close, n)

    def helper(e):
        return lax.rem(me + n - e * close, n)

    def remote(src, dst, send, recv, axis, to):
        return pltpu.make_async_remote_copy(
            src_ref=src, dst_ref=dst, send_sem=send, recv_sem=recv,
            device_id={axis: to}, device_id_type=MESH,
        )

    def fact_copy(k, to, slot):
        return remote(mine, facts.at[slot], fact_s.at[k], fact_r.at[k], "vis", to)

    def pair_copy(e, part):
        cut = pl.ds(part * (rt // 2), rt // 2)
        return remote(
            hold.at[1 if e == 2 else 0, cut], hold.at[e, cut],
            pair_s.at[2 * e + part], pair_r.at[2 * e + part], "vis", helper(1 if e == 2 else e),
        )

    def beam_copy(e):
        return remote(
            beams.at[1 if e == 2 else 0], beams.at[e], beam_s.at[e], beam_r.at[e],
            "vis", helper(1 if e == 2 else e),
        )

    def home_copy(e):
        return remote(
            total.at[e], homes.at[e], home_s.at[e], home_r.at[e],
            "vis", owner(me, 1 if e == 2 else e),
        )

    def msg_copy(s, e, k, to, slot):
        return remote(
            sends.at[s, e, to], got.at[s, slot], msg_s.at[s, e, k], msg_r.at[s, e, k], "vis", to
        )

    def back_copy(s, e, k, to, rows_of, slot):
        return remote(
            back_sends.at[s, rows_of], back.at[s, e, slot],
            back_s.at[s, e, k], back_r.at[s, e, k], "vis", to,
        )

    tall = rows * tay * fs // groups // lanes

    def sum_copy(r, to, slot):
        which = pl.ds(tall, (sets - 1) * tall) if r else pl.ds(0, tall)
        return remote(
            image.at[to, which], parts.at[slot, which],
            sum_s.at[r, to], sum_r.at[r, slot], "freq", to,
        )

    width = tay * fs // groups

    def out_copy(to, slot):
        place = dirty_ref.at[:, pl.ds(pl.multiple_of(slot * width, lanes), width)]
        return remote(result, place, out_s.at[to], out_r.at[slot], "freq", to)

    loads = [
        (off_hbm, off_ref),
        (w_hbm, w_ref),
        (beam_hbm, beam_ref),
        (model_hbm, model_ref),
        (uv_hbm, uv_ref),
        (sub_hbm, sub_ref),
        (fwd_hbm, t_fwd),
        (counts_hbm, counts_ref),
        (spec_hbm, spec_ref),
        (obs_hbm, obs_ref),
        (bwd_hbm, t_bwd),
    ]
    loads = [pltpu.make_async_copy(a, b, tab_sem.at[i]) for i, (a, b) in enumerate(loads)]
    for load in loads:
        load.start()
    barrier = pltpu.get_barrier_semaphore()

    def greet(axis, to):
        pl.semaphore_signal(barrier, inc=1, device_id={axis: to}, device_id_type=MESH)

    greet("vis", helper(1))
    greet("vis", helper(3))
    greet("vis", actor(close - 1))

    def greet_near(k, carry):
        greet("vis", other(close - k))
        return carry

    def greet_group(d, carry):
        greet("freq", lax.rem(group + d, groups))
        return carry

    lax.fori_loop(1, close, greet_near, 0)
    lax.fori_loop(1, groups, greet_group, 0)

    for load in loads[:4]:
        load.wait()
    lane = lax.broadcasted_iota(I32, (1, lanes), 1)
    fact = jnp.zeros((1, lanes), F32)
    for s in range(ns):
        fact = jnp.where(lane == s, off_ref[0, 0, 1, s].astype(F32), fact)
        fact = jnp.where(lane == ns + s, w_ref[0, 0, s].astype(F32), fact)
    mine[...] = fact
    gain = beam_ref[0].astype(F32)
    for t in range(tay):
        piece = (model_ref[:, t * fs : (t + 1) * fs].astype(F32) * gain).astype(BF)
        weighted[0, t * rows : (t + 1) * rows, :] = piece.astype(F32)
    hold[0] = weighted[0].astype(BF)
    beams[0] = jnp.concatenate([gain[:, : fs // 2], gain[:, fs // 2 :]], axis=0).astype(BF)

    pl.semaphore_wait(barrier, close + 2 + groups - 1)
    for e in (1, 3):
        for part in range(2):
            pair_copy(e, part).start()

    def tell(k, carry):
        fact_copy(k, actor(k), me).start()
        return carry

    lax.fori_loop(1, close, tell, 0)
    for e in (1, 3):
        beam_copy(e).start()
    facts[me] = mine[...]

    loads[6].wait()
    spot = lax.broadcasted_iota(I32, (qs, lanes), 0) * lanes + (
        lax.broadcasted_iota(I32, (qs, lanes), 1) - fs // 2
    )
    bits = 2 * log_fs + 1

    blocks = [other(u) for u in range(close)]

    def forward(e, s, carry):
        for u, j in enumerate(blocks):
            if e == 0:
                if s == 0 and u > 0:
                    fact_copy(u, j, j).wait_recv()
                told = facts[j].astype(I32)
                centre = jnp.broadcast_to(told[:, s : s + 1], (qs, lanes))
                plane = jnp.broadcast_to(told[:, ns + s : ns + s + 1], (qs, lanes))
                phase = phase_of(centre, spot, plane, log_fs)
                for c in range(2):
                    ramps[j, s, c] = cos_of(phase + (c << (bits - 2)), bits)
            for c in range(2):
                ramp = ramps[j, s, c]
                for q in range(qs):
                    cut = slice(q * lanes, (q + 1) * lanes)
                    at = c * fs + q * lanes
                    xbuf[u * rt : (u + 1) * rt, at : at + lanes] = (
                        weighted[e, :, cut] * ramp[q : q + 1, :]
                    ).astype(BF)
        proj = jnp.dot(xbuf[...], t_fwd[...], preferred_element_type=F32).astype(BF)
        for u, j in enumerate(blocks):
            sends[s, e, j] = proj[u * rt : (u + 1) * rt]
            if u > 0:
                msg_copy(s, e, u, j, owner(me, e)).start()
        got[s, owner(me, e)] = sends[s, e, me]
        return carry

    for s in range(ns):
        forward(0, s, 0)

    def row_factor(s, index, place):
        cell = off_ref[0, 0, 0, s] + (index & (S - 1)) - S // 2
        bits = 2 * log_ext + 1
        quarter = (index // S) << (bits - 2)
        return cos_of(phase_of(cell, place, w_ref[0, 0, s], log_ext) + quarter, bits).astype(BF)

    def place_of(shape, axis):
        return lax.broadcasted_iota(I32, shape, axis) - extent // 2

    shape = (wide, extent)
    turned = (extent, wide)
    for s in range(ns):
        eu[s] = row_factor(s, lax.broadcasted_iota(I32, shape, 0), place_of(shape, 1))
        eu_t[s] = row_factor(s, lax.broadcasted_iota(I32, turned, 1), place_of(turned, 0))

    loads[4].wait()
    loads[5].wait()
    step = min(512, nv)

    def kernels(i, carry):
        cut = pl.ds(pl.multiple_of(i * step, step), step)
        cells = lax.broadcasted_iota(I32, (S, step), 0).astype(F32)

        def table(position):
            d = position - cells
            return jnp.exp(d * d * (-0.5 / (KERNEL_WIDTH * KERNEL_WIDTH))).astype(BF).astype(F32)

        ku[:, cut] = table(uv_ref[0, 0, 0:1, cut])
        kv_all = table(uv_ref[0, 0, 1:2, cut])
        sub = sub_ref[0, :, cut]
        for s in range(ns):
            masked = jnp.where(sub == s, kv_all, 0.0).astype(BF)
            kv[s, :S, cut] = masked
            kv[s, S:, cut] = masked
        return carry

    lax.fori_loop(0, nv // step, kernels, 0)

    for part in range(2):
        pair_copy(1, part).wait_recv()
        pair_copy(2, part).start()
    for e in (1, 3, 2):
        if e > 1:
            for part in range(2):
                pair_copy(e, part).wait_recv()
        weighted[e] = hold[e].astype(F32)
        lax.fori_loop(0, ns, functools.partial(forward, e), 0)
        if e == 1:
            beam_copy(1).wait_recv()
            beam_copy(2).start()

    for load in loads[7:10]:
        load.wait()
    first = lax.broadcasted_iota(I32, (S, wide), 1) < S
    sign = jnp.where(first, -1.0, 1.0)

    for s in range(ns):

        def arrive(k, carry):
            j = actor(k)
            for e in range(sets):
                msg_copy(s, e, k, j, owner(j, e)).wait_recv()
            return carry

        lax.fori_loop(1, close, arrive, 0)

        for p in range(n // 2):
            one = got[s, 2 * p].astype(F32)
            two = got[s, 2 * p + 1].astype(F32)
            for t in range(tay):
                cut = slice(t * rows, (t + 1) * rows)
                both = jnp.concatenate([one[cut], two[cut]], axis=0).astype(BF)
                stage[t, 2 * rows * p : 2 * rows * (p + 1), :] = both
        for t in range(tay):
            prod = jnp.dot(eu[s], stage[t], preferred_element_type=F32)
            pair = prod[:S] + sign * pltpu.roll(prod[S:], S, 1)
            grid[2 * t * S : (2 * t + 1) * S, :] = jnp.where(first, pair, 0.0).astype(BF)
            grid[(2 * t + 1) * S : (2 * t + 2) * S, :] = jnp.where(first, 0.0, pair).astype(BF)

        gridded[...] = jnp.zeros_like(gridded)

        def visit(i, carry):
            cut = pl.ds(pl.multiple_of(i * step, step), step)
            ku_cut = ku[:, cut]
            kv_cut = kv[s, :, cut]
            spec = spec_ref[0, :, cut]
            powers = [jnp.ones_like(spec)]
            for t in range(1, tay):
                powers.append(powers[-1] * spec)
            cell = jnp.dot(grid[...], kv_cut, preferred_element_type=F32)
            number = lax.broadcasted_iota(I32, (1, step), 1) + i * step
            live = jnp.logical_and(number < counts_ref[0, 0], sub_ref[0, :, cut] == s)
            live = live.astype(F32)
            spread = []
            left = []
            for c in range(2):
                predicted = jnp.zeros((1, step), F32)
                for t in range(tay):
                    top = (2 * t + c) * S
                    part = jnp.sum(cell[top : top + S] * ku_cut, axis=0, keepdims=True)
                    predicted = predicted + part * powers[t]
                left.append(live * (obs_ref[0, 0, c : c + 1, cut] - predicted))
                if s == 0:
                    res_ref[0, 0, c : c + 1, cut] = left[c]
                else:
                    res_ref[0, 0, c : c + 1, cut] += left[c]
            for t in range(tay):
                for c in range(2):
                    spread.append(((left[c] * powers[t]) * ku_cut).astype(BF))
            spread = jnp.concatenate(spread, axis=0)
            gridded[...] += lax.dot_general(
                spread, kv_cut, (((1,), (1,)), ((), ())), preferred_element_type=F32
            )
            return carry

        lax.fori_loop(0, nv // step, visit, 0, unroll=True)

        for t in range(tay):
            re = gridded[2 * t * S : (2 * t + 1) * S, :]
            im = gridded[(2 * t + 1) * S : (2 * t + 2) * S, :]
            rhs = jnp.concatenate([jnp.where(first, re, im), jnp.where(first, im, -re)], axis=0)
            h[t] = jnp.dot(eu_t[s], rhs.astype(BF), preferred_element_type=F32)
        for j in range(n):
            back_sends[s, j] = jnp.concatenate(
                [h[t, j * rows : (j + 1) * rows, :] for t in range(tay)], axis=0
            ).astype(BF)

        for e in (2, 1, 3, 0):

            def give(k, carry):
                to = actor(k)
                back_copy(s, e, k, to, owner(to, e), me).start()
                return carry

            lax.fori_loop(1, close, give, 0)
        for e in range(sets):
            back[s, e, me] = back_sends[s, owner(me, e)]

    loads[10].wait()
    weighted[...] = jnp.zeros_like(weighted)
    norm_scale = 1.0 / (S * math.sqrt(groups * n * ns))
    per = groups // tay

    def peer(d):
        return lax.rem(group + d, groups)

    def gain_of(e):
        if e == 0:
            return gain
        if e > 1:
            beam_copy(e).wait_recv()
        far = beams[e].astype(F32)
        return jnp.concatenate([far[:rows], far[rows:]], axis=1)

    for s in range(ns):

        def collect(e, carry):
            for u, j in enumerate(blocks):
                if u > 0:
                    back_copy(s, e, u, j, owner(me, e), j).wait_recv()
            lhs = jnp.concatenate([back[s, e, j] for j in blocks], axis=0)
            for q in range(qs):
                z = jnp.dot(lhs, t_bwd[q], preferred_element_type=F32)
                cut = slice(q * lanes, (q + 1) * lanes)
                acc = weighted[e, :, cut]
                for u, j in enumerate(blocks):
                    for c in range(2):
                        ramp = ramps[j, s, c, q : q + 1, :]
                        part = z[u * rt : (u + 1) * rt, c * lanes : (c + 1) * lanes]
                        acc = acc + part * ramp
                weighted[e, :, cut] = acc
            return carry

        for r in (1, 0):
            acted = range(1, sets) if r else range(1)
            lax.fori_loop(acted.start, acted.stop, collect, 0)
            if s < ns - 1:
                continue
            for e in acted:
                scaled = gain_of(e) * norm_scale
                for f in range(groups):
                    t = f // per
                    for q in range(width // lanes):
                        at = (f % per) * width + q * lanes
                        cut = slice(at, at + lanes)
                        top = e * tall + q * rows
                        stage_f32[f, top : top + rows, :] = (
                            weighted[e, t * rows : (t + 1) * rows, cut] * scaled[:, cut]
                        )
            low, high = acted.start * tall, acted.stop * tall
            image[:, low:high, :] = stage_f32[:, low:high, :].astype(BF)

            def share(d, carry):
                sum_copy(r, peer(d), group).start()
                return carry

            lax.fori_loop(1, groups, share, 0)

    for r in (1, 0):
        acted = range(1, sets) if r else range(1)
        low, high = acted.start * tall, acted.stop * tall

        def add(d, running):
            j = peer(d)
            sum_copy(r, j, j).wait_recv()
            return running + parts[j, low:high, :].astype(F32)

        summed = lax.fori_loop(1, groups, add, stage_f32[group, low:high, :])
        for e in acted:
            total[e] = summed[e * tall - low : (e + 1) * tall - low]
            if e > 1:
                home_copy(e).start()
        if r == 1:
            home_copy(2).wait_recv()
            total[1] += homes[2]
            home_copy(1).start()
    whole = total[0]
    for e in (3, 1):
        home_copy(e).wait_recv()
        whole = whole + homes[e]
    pieces = [whole[q * rows : (q + 1) * rows] for q in range(width // lanes)]
    result[...] = jnp.concatenate(pieces, axis=1)

    def publish(d, carry):
        out_copy(peer(d), group).start()
        return carry

    lax.fori_loop(1, groups, publish, 0)
    dirty_ref[:, pl.ds(pl.multiple_of(group * width, lanes), width)] = result[...]

    for e in range(1, sets):
        for part in range(2):
            pair_copy(e, part).wait_send()
        beam_copy(e).wait_send()
        home_copy(e).wait_send()

    def finish(k, carry):
        to = other(k)
        of = actor(k)
        fact_copy(k, of, me).wait_send()
        for s in range(ns):
            for e in range(sets):
                msg_copy(s, e, k, to, me).wait_send()
        return carry

    lax.fori_loop(1, close, finish, 0)

    def finish_back(k, carry):
        of = actor(k)
        for s in range(ns):
            for e in range(sets):
                back_copy(s, e, k, of, owner(of, e), me).wait_send()
        return carry

    lax.fori_loop(1, close, finish_back, 0)

    def close(d, carry):
        j = peer(d)
        for r in range(2):
            sum_copy(r, j, group).wait_send()
        out_copy(j, group).wait_send()
        out_copy(j, j).wait_recv()
        return carry

    lax.fori_loop(1, groups, close, 0)


def shards(model, beam, vis_obs, vis_uv, spectral, vis_subgrid, counts, uv_offsets, w_planes):
    rows = model.shape[0]
    fs = beam.shape[-1]
    tay = model.shape[1] // fs
    n = lax.axis_size("vis")
    groups = lax.axis_size("freq")
    extent = rows * n
    ns = w_planes.shape[-1]
    nv = vis_obs.shape[-1]
    rt = tay * rows
    wide = 2 * S
    lanes = 128
    qs = fs // lanes

    t_re, t_im = dft_tables(fs)
    fwd = np.concatenate(
        [np.concatenate([t_re.T, t_im.T], 1), np.concatenate([-t_im.T, t_re.T], 1)], 0
    )
    split = (S, qs, 1, lanes)
    re, im = t_re.reshape(split), t_im.reshape(split)
    bwd = np.concatenate(
        [np.concatenate([re, -im], 2), np.concatenate([im, re], 2)], 0
    )
    bwd = bwd.reshape(2 * S, qs, 2 * lanes).transpose(1, 0, 2)

    tall = rows * tay * fs // groups // lanes
    dma = pltpu.SemaphoreType.DMA
    vmem = pl.BlockSpec(memory_space=pltpu.VMEM)
    hbm = pl.BlockSpec(memory_space=pltpu.HBM)
    dims = (n, groups, tay, rows, fs, ns, nv)
    return pl.pallas_call(
        functools.partial(whole_kernel, dims),
        name="whole",
        out_shape=(
            jax.ShapeDtypeStruct((1, 1, 2, nv), F32),
            jax.ShapeDtypeStruct((rows, tay * fs), F32),
        ),
        in_specs=[hbm] * 11,
        out_specs=(vmem, vmem),
        scratch_shapes=[
            pltpu.VMEM((rows, tay * fs), BF),
            pltpu.VMEM((1, rows, fs), BF),
            pltpu.VMEM((1, 1, 2, nv), F32),
            pltpu.VMEM((1, 1, 2, nv), F32),
            pltpu.VMEM((1, 1, nv), F32),
            pltpu.VMEM((1, 1, nv), I32),
            pltpu.SMEM((1, 1), I32),
            pltpu.SMEM((1, 1, 2, ns), I32),
            pltpu.SMEM((1, 1, ns), I32),
            pltpu.VMEM((2 * fs, wide), BF),
            pltpu.VMEM((qs, wide, 2 * lanes), BF),
            pltpu.VMEM((1, lanes), F32),
            pltpu.VMEM((n, 1, lanes), F32),
            pltpu.VMEM((n, ns, 2, qs, lanes), F32),
            pltpu.VMEM((4, rt, fs), BF),
            pltpu.VMEM((4, 2 * rows, fs // 2), BF),
            pltpu.VMEM((4, rt, fs), F32),
            pltpu.VMEM((8 * rt, 2 * fs), BF),
            pltpu.VMEM((ns, 4, n, rt, wide), BF),
            pltpu.VMEM((ns, n, rt, wide), BF),
            pltpu.VMEM((tay, extent, wide), BF),
            pltpu.VMEM((ns, wide, extent), BF),
            pltpu.VMEM((ns, extent, wide), BF),
            pltpu.VMEM((S, nv), F32),
            pltpu.VMEM((ns, wide, nv), BF),
            pltpu.VMEM((2 * tay * S, wide), BF),
            pltpu.VMEM((2 * tay * S, wide), F32),
            pltpu.VMEM((tay, extent, wide), F32),
            pltpu.VMEM((ns, n, rt, wide), BF),
            pltpu.VMEM((ns, 4, n, rt, wide), BF),
            pltpu.VMEM((groups, 4 * tall, lanes), BF),
            pltpu.VMEM((groups, 4 * tall, lanes), BF),
            pltpu.VMEM((groups, 4 * tall, lanes), F32),
            pltpu.VMEM((4, tall, lanes), F32),
            pltpu.VMEM((4, tall, lanes), F32),
            pltpu.VMEM((rows, tay * fs // groups), F32),
            dma((11,)),
            dma((n // 4,)), dma((n // 4,)),
            dma((8,)), dma((8,)),
            dma((4,)), dma((4,)),
            dma((4,)), dma((4,)),
            dma((ns, 4, n // 4)), dma((ns, 4, n // 4)),
            dma((ns, 4, n // 4)), dma((ns, 4, n // 4)),
            dma((2, groups)), dma((2, groups)),
            dma((groups,)), dma((groups,)),
        ],
        compiler_params=pltpu.CompilerParams(
            collective_id=0, has_side_effects=True, vmem_limit_bytes=60 * 2**20
        ),
    )(
        model, beam, vis_obs, vis_uv, spectral, vis_subgrid, counts, uv_offsets, w_planes,
        np.ascontiguousarray(fwd).astype(BF), np.ascontiguousarray(bwd).astype(BF),
    )


def solution(mesh):
    in_specs = (
        P("vis", None),
        P("freq", "vis", None),
        P("freq", "vis", None, None),
        P("freq", "vis", None, None),
        P("freq", "vis", None),
        P("freq", "vis", None),
        P("freq", "vis"),
        P("freq", "vis", None, None),
        P("freq", "vis", None),
    )
    out_specs = (P("freq", "vis", None, None), P("vis", None))
    return jax.shard_map(shards, mesh=mesh, in_specs=in_specs, out_specs=out_specs, check_vma=False)
```

```python
import functools
import math

import jax
import jax.numpy as jnp
import numpy as np
from jax import lax
from jax.experimental import pallas as pl
from jax.experimental.pallas import tpu as pltpu
from jax.sharding import PartitionSpec as P

S = 64
KERNEL_WIDTH = 0.5
MESH = pl.DeviceIdType.MESH
BF = jnp.bfloat16
F32 = jnp.float32
I32 = jnp.int32


def dft_tables(pixels):
    cells = np.arange(S) - S // 2
    places = np.arange(pixels) - pixels // 2
    angle = -2.0 * np.pi * np.mod(cells[:, None] * places[None, :], pixels) / pixels
    return np.cos(angle).astype(np.float32), np.sin(angle).astype(np.float32)


def cos_of(phase, bits):
    full = 1 << bits
    phase = phase & (full - 1)
    phase = jnp.where(phase >= full // 2, full - phase, phase)
    x = (0.25 - phase.astype(F32) * (1.0 / full)) * (2.0 * math.pi)
    y = x * x
    total = jnp.full_like(x, -1.0 / math.factorial(11))
    for power in (9, 7, 5, 3, 1):
        sign = 1.0 if power % 4 == 1 else -1.0
        total = total * y + sign / math.factorial(power)
    return total * x


def phase_of(cell, place, w_plane, log2):
    pixels = 1 << log2
    linear = (cell * place) & (pixels - 1)
    quadratic = (w_plane * place * place) & (2 * pixels * pixels - 1)
    return (linear << (log2 + 1)) + quadratic


def offset(k):
    return ((k + 1) // 2) * (1 - 2 * ((k + 1) % 2))


def whole_kernel(
    dims,
    model_hbm, beam_hbm, obs_hbm, uv_hbm, spec_hbm, sub_hbm, counts_hbm, off_hbm, w_hbm,
    fwd_hbm, bwd_hbm,
    res_hbm, dirty_hbm,
    res_ref, model_ref, beam_ref, obs_ref, uv_ref, spec_ref, sub_ref, counts_ref, off_ref, w_ref,
    t_fwd, t_bwd, mine, facts, ramps, hold, beams, weighted,
    xbuf, sends, got, stage, eu, eu_t, ku, kv, grid, gridded, h, back_sends, back, image, parts,
    stage_f32, total, homes, result,
    tab_sem, fact_s, fact_r, pair_s, pair_r, beam_s, beam_r, home_s, home_r,
    msg_s, msg_r, back_s, back_r, sum_s, sum_r, out_s, out_r,
):
    n, groups, tay, rows, fs, ns, nv = dims
    rt = tay * rows
    extent = n * rows
    log_fs = fs.bit_length() - 1
    log_ext = extent.bit_length() - 1
    lanes = 128
    wide = 2 * S
    qs = fs // lanes
    me = lax.axis_index("vis")
    group = lax.axis_index("freq")

    sets = 4
    close = n // sets

    def other(k):
        return lax.rem(me + offset(k) + n, n)

    def actor(k):
        return lax.rem(me - offset(k) + n, n)

    def owner(device, e):
        return lax.rem(device + e * close, n)

    def helper(e):
        return lax.rem(me + n - e * close, n)

    def remote(src, dst, send, recv, axis, to):
        return pltpu.make_async_remote_copy(
            src_ref=src, dst_ref=dst, send_sem=send, recv_sem=recv,
            device_id={axis: to}, device_id_type=MESH,
        )

    def fact_copy(k, to, slot):
        return remote(mine, facts.at[slot], fact_s.at[k], fact_r.at[k], "vis", to)

    def pair_copy(e, part):
        cut = pl.ds(part * (rt // 2), rt // 2)
        way = e if e != 2 else (1, 3)[part]
        return remote(
            hold.at[way if e == 2 else 0, cut], hold.at[e, cut],
            pair_s.at[2 * e + part], pair_r.at[2 * e + part], "vis", helper(way),
        )

    def beam_copy(e):
        return remote(
            beams.at[1 if e == 2 else 0], beams.at[e], beam_s.at[e], beam_r.at[e],
            "vis", helper(1 if e == 2 else e),
        )

    def home_copy(e):
        return remote(
            total.at[e], homes.at[e], home_s.at[e], home_r.at[e],
            "vis", owner(me, 1 if e == 2 else e),
        )

    def msg_copy(s, e, k, to, slot):
        return remote(
            sends.at[s, e, to], got.at[s, slot], msg_s.at[s, e, k], msg_r.at[s, e, k], "vis", to
        )

    def back_copy(s, e, k, to, rows_of, slot):
        return remote(
            back_sends.at[s, rows_of], back.at[s, e, slot],
            back_s.at[s, e, k], back_r.at[s, e, k], "vis", to,
        )

    tall = rows * tay * fs // groups // lanes

    def sum_copy(r, to, slot):
        which = pl.ds(tall, (sets - 1) * tall) if r else pl.ds(0, tall)
        return remote(
            image.at[to, which], parts.at[slot, which],
            sum_s.at[r, to], sum_r.at[r, slot], "freq", to,
        )

    width = tay * fs // groups

    def out_copy(to, slot):
        place = dirty_hbm.at[:, pl.ds(pl.multiple_of(slot * width, lanes), width)]
        return remote(result, place, out_s.at[to], out_r.at[slot], "freq", to)

    loads = [
        (off_hbm, off_ref),
        (w_hbm, w_ref),
        (beam_hbm, beam_ref),
        (model_hbm, model_ref),
        (uv_hbm, uv_ref),
        (sub_hbm, sub_ref),
        (fwd_hbm, t_fwd),
        (counts_hbm, counts_ref),
        (spec_hbm, spec_ref),
        (obs_hbm, obs_ref),
        (bwd_hbm, t_bwd),
    ]
    loads = [pltpu.make_async_copy(a, b, tab_sem.at[i]) for i, (a, b) in enumerate(loads)]
    for load in loads:
        load.start()
    barrier = pltpu.get_barrier_semaphore()

    def greet(axis, to):
        pl.semaphore_signal(barrier, inc=1, device_id={axis: to}, device_id_type=MESH)

    greet("vis", helper(1))
    greet("vis", helper(3))
    greet("vis", actor(close - 1))

    def greet_near(k, carry):
        greet("vis", other(close - k))
        return carry

    def greet_group(d, carry):
        greet("freq", lax.rem(group + d, groups))
        return carry

    lax.fori_loop(1, close, greet_near, 0)
    lax.fori_loop(1, groups, greet_group, 0)

    for load in loads[:4]:
        load.wait()
    lane = lax.broadcasted_iota(I32, (1, lanes), 1)
    fact = jnp.zeros((1, lanes), F32)
    for s in range(ns):
        fact = jnp.where(lane == s, off_ref[0, 0, 1, s].astype(F32), fact)
        fact = jnp.where(lane == ns + s, w_ref[0, 0, s].astype(F32), fact)
    mine[...] = fact
    gain = beam_ref[0].astype(F32)
    for t in range(tay):
        piece = (model_ref[:, t * fs : (t + 1) * fs].astype(F32) * gain).astype(BF)
        weighted[0, t * rows : (t + 1) * rows, :] = piece.astype(F32)
    hold[0] = weighted[0].astype(BF)
    beams[0] = jnp.concatenate([gain[:, : fs // 2], gain[:, fs // 2 :]], axis=0).astype(BF)

    pl.semaphore_wait(barrier, close + 2 + groups - 1)
    for e, part in ((1, 0), (3, 1), (1, 1), (3, 0)):
        pair_copy(e, part).start()

    def tell(k, carry):
        fact_copy(k, actor(k), me).start()
        return carry

    lax.fori_loop(1, close, tell, 0)
    for e in (1, 3):
        beam_copy(e).start()
    facts[me] = mine[...]

    loads[6].wait()
    spot = lax.broadcasted_iota(I32, (qs, lanes), 0) * lanes + (
        lax.broadcasted_iota(I32, (qs, lanes), 1) - fs // 2
    )
    bits = 2 * log_fs + 1

    blocks = [other(u) for u in range(close)]

    def forward(e, s, carry):
        for u, j in enumerate(blocks):
            if e == 0:
                if s == 0 and u > 0:
                    fact_copy(u, j, j).wait_recv()
                told = facts[j].astype(I32)
                centre = jnp.broadcast_to(told[:, s : s + 1], (qs, lanes))
                plane = jnp.broadcast_to(told[:, ns + s : ns + s + 1], (qs, lanes))
                phase = phase_of(centre, spot, plane, log_fs)
                for c in range(2):
                    ramps[j, s, c] = cos_of(phase + (c << (bits - 2)), bits)
            for c in range(2):
                ramp = ramps[j, s, c]
                for q in range(qs):
                    cut = slice(q * lanes, (q + 1) * lanes)
                    at = c * fs + q * lanes
                    xbuf[u * rt : (u + 1) * rt, at : at + lanes] = (
                        weighted[e, :, cut] * ramp[q : q + 1, :]
                    ).astype(BF)
        proj = jnp.dot(xbuf[...], t_fwd[...], preferred_element_type=F32).astype(BF)
        for u, j in enumerate(blocks):
            sends[s, e, j] = proj[u * rt : (u + 1) * rt]
            if u > 0:
                msg_copy(s, e, u, j, owner(me, e)).start()
        got[s, owner(me, e)] = sends[s, e, me]
        return carry

    for s in range(ns):
        forward(0, s, 0)

    def row_factor(s, index, place):
        cell = off_ref[0, 0, 0, s] + (index & (S - 1)) - S // 2
        bits = 2 * log_ext + 1
        quarter = (index // S) << (bits - 2)
        return cos_of(phase_of(cell, place, w_ref[0, 0, s], log_ext) + quarter, bits).astype(BF)

    def place_of(shape, axis):
        return lax.broadcasted_iota(I32, shape, axis) - extent // 2

    shape = (wide, extent)
    turned = (extent, wide)
    for s in range(ns):
        eu[s] = row_factor(s, lax.broadcasted_iota(I32, shape, 0), place_of(shape, 1))
        eu_t[s] = row_factor(s, lax.broadcasted_iota(I32, turned, 1), place_of(turned, 0))

    loads[4].wait()
    loads[5].wait()
    step = min(512, nv)

    def kernels(i, carry):
        cut = pl.ds(pl.multiple_of(i * step, step), step)
        cells = lax.broadcasted_iota(I32, (S, step), 0).astype(F32)

        def table(position):
            d = position - cells
            return jnp.exp(d * d * (-0.5 / (KERNEL_WIDTH * KERNEL_WIDTH))).astype(BF).astype(F32)

        ku[:, cut] = table(uv_ref[0, 0, 0:1, cut])
        kv_all = table(uv_ref[0, 0, 1:2, cut])
        sub = sub_ref[0, :, cut]
        for s in range(ns):
            masked = jnp.where(sub == s, kv_all, 0.0).astype(BF)
            kv[s, :S, cut] = masked
            kv[s, S:, cut] = masked
        return carry

    lax.fori_loop(0, nv // step, kernels, 0)

    for part, e in ((0, 1), (1, 3)):
        pair_copy(e, part).wait_recv()
        pair_copy(2, part).start()
    for e in (1, 3, 2):
        for part in range(2):
            if (e, part) not in ((1, 0), (3, 1)):
                pair_copy(e, part).wait_recv()
        weighted[e] = hold[e].astype(F32)
        lax.fori_loop(0, ns, functools.partial(forward, e), 0)
        if e == 1:
            beam_copy(1).wait_recv()
            beam_copy(2).start()

    for load in loads[7:10]:
        load.wait()
    first = lax.broadcasted_iota(I32, (S, wide), 1) < S
    sign = jnp.where(first, -1.0, 1.0)

    for s in range(ns):

        def arrive(k, carry):
            j = actor(k)
            for e in range(sets):
                msg_copy(s, e, k, j, owner(j, e)).wait_recv()
            return carry

        lax.fori_loop(1, close, arrive, 0)

        for p in range(n // 2):
            one = got[s, 2 * p].astype(F32)
            two = got[s, 2 * p + 1].astype(F32)
            for t in range(tay):
                cut = slice(t * rows, (t + 1) * rows)
                both = jnp.concatenate([one[cut], two[cut]], axis=0).astype(BF)
                stage[t, 2 * rows * p : 2 * rows * (p + 1), :] = both
        for t in range(tay):
            prod = jnp.dot(eu[s], stage[t], preferred_element_type=F32)
            pair = prod[:S] + sign * pltpu.roll(prod[S:], S, 1)
            grid[2 * t * S : (2 * t + 1) * S, :] = jnp.where(first, pair, 0.0).astype(BF)
            grid[(2 * t + 1) * S : (2 * t + 2) * S, :] = jnp.where(first, 0.0, pair).astype(BF)

        gridded[...] = jnp.zeros_like(gridded)

        def visit(i, carry):
            cut = pl.ds(pl.multiple_of(i * step, step), step)
            ku_cut = ku[:, cut]
            kv_cut = kv[s, :, cut]
            spec = spec_ref[0, :, cut]
            powers = [jnp.ones_like(spec)]
            for t in range(1, tay):
                powers.append(powers[-1] * spec)
            cell = jnp.dot(grid[...], kv_cut, preferred_element_type=F32)
            number = lax.broadcasted_iota(I32, (1, step), 1) + i * step
            live = jnp.logical_and(number < counts_ref[0, 0], sub_ref[0, :, cut] == s)
            live = live.astype(F32)
            spread = []
            left = []
            for c in range(2):
                predicted = jnp.zeros((1, step), F32)
                for t in range(tay):
                    top = (2 * t + c) * S
                    part = jnp.sum(cell[top : top + S] * ku_cut, axis=0, keepdims=True)
                    predicted = predicted + part * powers[t]
                left.append(live * (obs_ref[0, 0, c : c + 1, cut] - predicted))
                if s == 0:
                    res_ref[0, 0, c : c + 1, cut] = left[c]
                else:
                    res_ref[0, 0, c : c + 1, cut] += left[c]
            for t in range(tay):
                for c in range(2):
                    spread.append(((left[c] * powers[t]) * ku_cut).astype(BF))
            spread = jnp.concatenate(spread, axis=0)
            gridded[...] += lax.dot_general(
                spread, kv_cut, (((1,), (1,)), ((), ())), preferred_element_type=F32
            )
            return carry

        lax.fori_loop(0, nv // step, visit, 0, unroll=True)

        for t in range(tay):
            re = gridded[2 * t * S : (2 * t + 1) * S, :]
            im = gridded[(2 * t + 1) * S : (2 * t + 2) * S, :]
            rhs = jnp.concatenate([jnp.where(first, re, im), jnp.where(first, im, -re)], axis=0)
            h[t] = jnp.dot(eu_t[s], rhs.astype(BF), preferred_element_type=F32)
        for j in range(n):
            back_sends[s, j] = jnp.concatenate(
                [h[t, j * rows : (j + 1) * rows, :] for t in range(tay)], axis=0
            ).astype(BF)

        for e in (2, 1, 3, 0):

            def give(k, carry):
                to = actor(k)
                back_copy(s, e, k, to, owner(to, e), me).start()
                return carry

            lax.fori_loop(1, close, give, 0)
        for e in range(sets):
            back[s, e, me] = back_sends[s, owner(me, e)]

    res_copy = pltpu.make_async_copy(res_ref, res_hbm, tab_sem.at[11])
    res_copy.start()

    loads[10].wait()
    weighted[...] = jnp.zeros_like(weighted)
    norm_scale = 1.0 / (S * math.sqrt(groups * n * ns))
    per = groups // tay

    def peer(d):
        return lax.rem(group + d, groups)

    def gain_of(e):
        if e == 0:
            return gain
        if e > 1:
            beam_copy(e).wait_recv()
        far = beams[e].astype(F32)
        return jnp.concatenate([far[:rows], far[rows:]], axis=1)

    for s in range(ns):

        def collect(e, carry):
            for u, j in enumerate(blocks):
                if u > 0:
                    back_copy(s, e, u, j, owner(me, e), j).wait_recv()
            lhs = jnp.concatenate([back[s, e, j] for j in blocks], axis=0)
            for q in range(qs):
                z = jnp.dot(lhs, t_bwd[q], preferred_element_type=F32)
                cut = slice(q * lanes, (q + 1) * lanes)
                acc = weighted[e, :, cut]
                for u, j in enumerate(blocks):
                    for c in range(2):
                        ramp = ramps[j, s, c, q : q + 1, :]
                        part = z[u * rt : (u + 1) * rt, c * lanes : (c + 1) * lanes]
                        acc = acc + part * ramp
                weighted[e, :, cut] = acc
            return carry

        for r in (1, 0):
            acted = range(1, sets) if r else range(1)
            lax.fori_loop(acted.start, acted.stop, collect, 0)
            if s < ns - 1:
                continue
            for e in acted:
                scaled = gain_of(e) * norm_scale
                for f in range(groups):
                    t = f // per
                    for q in range(width // lanes):
                        at = (f % per) * width + q * lanes
                        cut = slice(at, at + lanes)
                        top = e * tall + q * rows
                        stage_f32[f, top : top + rows, :] = (
                            weighted[e, t * rows : (t + 1) * rows, cut] * scaled[:, cut]
                        )
            low, high = acted.start * tall, acted.stop * tall
            image[:, low:high, :] = stage_f32[:, low:high, :].astype(BF)

            def share(d, carry):
                sum_copy(r, peer(d), group).start()
                return carry

            lax.fori_loop(1, groups, share, 0)

    for r in (1, 0):
        acted = range(1, sets) if r else range(1)
        low, high = acted.start * tall, acted.stop * tall

        def add(d, running):
            j = peer(d)
            sum_copy(r, j, j).wait_recv()
            return running + parts[j, low:high, :].astype(F32)

        summed = lax.fori_loop(1, groups, add, stage_f32[group, low:high, :])
        for e in acted:
            total[e] = summed[e * tall - low : (e + 1) * tall - low]
            if e > 1:
                home_copy(e).start()
        if r == 1:
            home_copy(2).wait_recv()
            total[1] += homes[2]
            home_copy(1).start()
    whole = total[0]
    for e in (3, 1):
        home_copy(e).wait_recv()
        whole = whole + homes[e]
    pieces = [whole[q * rows : (q + 1) * rows] for q in range(width // lanes)]
    result[...] = jnp.concatenate(pieces, axis=1)

    def publish(d, carry):
        out_copy(peer(d), group).start()
        return carry

    lax.fori_loop(1, groups, publish, 0)
    place = dirty_hbm.at[:, pl.ds(pl.multiple_of(group * width, lanes), width)]
    own_copy = pltpu.make_async_copy(result, place, tab_sem.at[12])
    own_copy.start()

    for e in range(1, sets):
        for part in range(2):
            pair_copy(e, part).wait_send()
        beam_copy(e).wait_send()
        home_copy(e).wait_send()

    def finish(k, carry):
        to = other(k)
        of = actor(k)
        fact_copy(k, of, me).wait_send()
        for s in range(ns):
            for e in range(sets):
                msg_copy(s, e, k, to, me).wait_send()
        return carry

    lax.fori_loop(1, close, finish, 0)

    def finish_back(k, carry):
        of = actor(k)
        for s in range(ns):
            for e in range(sets):
                back_copy(s, e, k, of, owner(of, e), me).wait_send()
        return carry

    lax.fori_loop(1, close, finish_back, 0)

    def close(d, carry):
        j = peer(d)
        for r in range(2):
            sum_copy(r, j, group).wait_send()
        out_copy(j, group).wait_send()
        out_copy(j, j).wait_recv()
        return carry

    lax.fori_loop(1, groups, close, 0)
    own_copy.wait()
    res_copy.wait()


def shards(model, beam, vis_obs, vis_uv, spectral, vis_subgrid, counts, uv_offsets, w_planes):
    rows = model.shape[0]
    fs = beam.shape[-1]
    tay = model.shape[1] // fs
    n = lax.axis_size("vis")
    groups = lax.axis_size("freq")
    extent = rows * n
    ns = w_planes.shape[-1]
    nv = vis_obs.shape[-1]
    rt = tay * rows
    wide = 2 * S
    lanes = 128
    qs = fs // lanes

    t_re, t_im = dft_tables(fs)
    fwd = np.concatenate(
        [np.concatenate([t_re.T, t_im.T], 1), np.concatenate([-t_im.T, t_re.T], 1)], 0
    )
    split = (S, qs, 1, lanes)
    re, im = t_re.reshape(split), t_im.reshape(split)
    bwd = np.concatenate(
        [np.concatenate([re, -im], 2), np.concatenate([im, re], 2)], 0
    )
    bwd = bwd.reshape(2 * S, qs, 2 * lanes).transpose(1, 0, 2)

    tall = rows * tay * fs // groups // lanes
    dma = pltpu.SemaphoreType.DMA
    hbm = pl.BlockSpec(memory_space=pltpu.HBM)
    dims = (n, groups, tay, rows, fs, ns, nv)
    return pl.pallas_call(
        functools.partial(whole_kernel, dims),
        name="whole",
        out_shape=(
            jax.ShapeDtypeStruct((1, 1, 2, nv), F32),
            jax.ShapeDtypeStruct((rows, tay * fs), F32),
        ),
        in_specs=[hbm] * 11,
        out_specs=(hbm, hbm),
        scratch_shapes=[
            pltpu.VMEM((1, 1, 2, nv), F32),
            pltpu.VMEM((rows, tay * fs), BF),
            pltpu.VMEM((1, rows, fs), BF),
            pltpu.VMEM((1, 1, 2, nv), F32),
            pltpu.VMEM((1, 1, 2, nv), F32),
            pltpu.VMEM((1, 1, nv), F32),
            pltpu.VMEM((1, 1, nv), I32),
            pltpu.SMEM((1, 1), I32),
            pltpu.SMEM((1, 1, 2, ns), I32),
            pltpu.SMEM((1, 1, ns), I32),
            pltpu.VMEM((2 * fs, wide), BF),
            pltpu.VMEM((qs, wide, 2 * lanes), BF),
            pltpu.VMEM((1, lanes), F32),
            pltpu.VMEM((n, 1, lanes), F32),
            pltpu.VMEM((n, ns, 2, qs, lanes), F32),
            pltpu.VMEM((4, rt, fs), BF),
            pltpu.VMEM((4, 2 * rows, fs // 2), BF),
            pltpu.VMEM((4, rt, fs), F32),
            pltpu.VMEM((8 * rt, 2 * fs), BF),
            pltpu.VMEM((ns, 4, n, rt, wide), BF),
            pltpu.VMEM((ns, n, rt, wide), BF),
            pltpu.VMEM((tay, extent, wide), BF),
            pltpu.VMEM((ns, wide, extent), BF),
            pltpu.VMEM((ns, extent, wide), BF),
            pltpu.VMEM((S, nv), F32),
            pltpu.VMEM((ns, wide, nv), BF),
            pltpu.VMEM((2 * tay * S, wide), BF),
            pltpu.VMEM((2 * tay * S, wide), F32),
            pltpu.VMEM((tay, extent, wide), F32),
            pltpu.VMEM((ns, n, rt, wide), BF),
            pltpu.VMEM((ns, 4, n, rt, wide), BF),
            pltpu.VMEM((groups, 4 * tall, lanes), BF),
            pltpu.VMEM((groups, 4 * tall, lanes), BF),
            pltpu.VMEM((groups, 4 * tall, lanes), F32),
            pltpu.VMEM((4, tall, lanes), F32),
            pltpu.VMEM((4, tall, lanes), F32),
            pltpu.VMEM((rows, tay * fs // groups), F32),
            dma((13,)),
            dma((n // 4,)), dma((n // 4,)),
            dma((8,)), dma((8,)),
            dma((4,)), dma((4,)),
            dma((4,)), dma((4,)),
            dma((ns, 4, n // 4)), dma((ns, 4, n // 4)),
            dma((ns, 4, n // 4)), dma((ns, 4, n // 4)),
            dma((2, groups)), dma((2, groups)),
            dma((groups,)), dma((groups,)),
        ],
        compiler_params=pltpu.CompilerParams(
            collective_id=0, has_side_effects=True, vmem_limit_bytes=60 * 2**20
        ),
    )(
        model, beam, vis_obs, vis_uv, spectral, vis_subgrid, counts, uv_offsets, w_planes,
        np.ascontiguousarray(fwd).astype(BF), np.ascontiguousarray(bwd).astype(BF),
    )


def solution(mesh):
    in_specs = (
        P("vis", None),
        P("freq", "vis", None),
        P("freq", "vis", None, None),
        P("freq", "vis", None, None),
        P("freq", "vis", None),
        P("freq", "vis", None),
        P("freq", "vis"),
        P("freq", "vis", None, None),
        P("freq", "vis", None),
    )
    out_specs = (P("freq", "vis", None, None), P("vis", None))
    return jax.shard_map(shards, mesh=mesh, in_specs=in_specs, out_specs=out_specs, check_vma=False)
```
